512 devices in a mesh: dp: 2 (over core), tensor: 16 (over z), context: 16 (over y, x).
Axes of the slice: x: 4, y: 4, z: 16, core: 2. Of those that a mesh axis runs over, the one named last changes fastest.
Arguments:
- teacher_hidden: bfloat16 [2048, 4096], P(('dp', 'context')), may hold values from -48 to 48
- draft_hidden: bfloat16 [2048, 2048], P(('dp', 'context')), may hold values from -48 to 48
- teacher_head: bfloat16 [4096, 65536], P(None, ('tensor', 'context')), may hold values from -0.484375 to 0.484375
- draft_head: bfloat16 [2048, 65536], P(None, ('tensor', 'context')), may hold values from -0.6850097 to 0.6850097
Outputs:
- token_kl: float32 [2048], P(('dp', 'context'))
- head_grad: bfloat16 [2048, 65536], P('dp', ('tensor', 'context'))
The draws below stay inside these ranges and needn't reach their ends.
All inputs are finite; a program needn't handle non-finite values.
Results may differ from the reference program's by a relative error of at most 0.0049.
Values may be sent and summed in bfloat16 or wider, within the bound.
A program may use at most 128 MiB of HBM per device.

```python
import math
import jax
import jax.numpy as jnp
from jax import lax

D = 4096
DD = 2048
VOCAB = 65536
TOKENS = 2048


def column_scale(key, index, total):
    spread = jax.random.uniform(jax.random.fold_in(key, index), (), jnp.float32)
    ramp = 0.8 + 0.4 * index.astype(jnp.float32) / total
    return jnp.exp(math.log(0.5) + (math.log(1.6) - math.log(0.5)) * spread) * ramp


def head_column(key, index, width, total):
    normals = jax.random.normal(jax.random.fold_in(jax.random.fold_in(key, 1), index), (width,), jnp.float32)
    entries = jnp.clip(normals, -4.0, 4.0) * (4.0 / math.sqrt(width))
    return entries * column_scale(jax.random.fold_in(key, 2), index, total)


def head_matrix(key, width, total):
    indices = jnp.arange(total, dtype=jnp.int32)
    columns = jax.vmap(lambda index: head_column(key, index, width, total))(indices)
    return columns.T


def hidden_rows(key, salt, width):
    own_key = jax.random.fold_in(key, salt)
    row_scale = jnp.exp(jax.random.uniform(jax.random.fold_in(own_key, 1), (TOKENS, 1), jnp.float32, math.log(0.5), math.log(1.6)))
    values = jnp.clip(jax.random.normal(jax.random.fold_in(own_key, 2), (TOKENS, width), jnp.float32), -5.0, 5.0) * row_scale
    return jnp.clip(values, -48.0, 48.0)


def draw_teacher_hidden(key, part):
    return hidden_rows(key, 21, D).astype(jnp.bfloat16)


def draw_draft_hidden(key, part):
    return hidden_rows(key, 31, DD).astype(jnp.bfloat16)


def draw_teacher_head(key, part):
    return head_matrix(jax.random.fold_in(key, 11), D, VOCAB).astype(jnp.bfloat16)


def draw_draft_head(key, part):
    return head_matrix(jax.random.fold_in(key, 12), DD, VOCAB).astype(jnp.bfloat16)


def setup_inputs(seed: int = 0) -> dict:
    keys = jax.random.split(jax.random.key(seed), 5)
    teacher_hidden = draw_teacher_hidden(jax.random.fold_in(keys[4], 71), 0)
    draft_hidden = draw_draft_hidden(jax.random.fold_in(keys[4], 71), 0)
    teacher_head = draw_teacher_head(jax.random.fold_in(keys[4], 71), 0)
    draft_head = draw_draft_head(jax.random.fold_in(keys[4], 71), 0)
    return {"teacher_hidden": teacher_hidden, "draft_hidden": draft_hidden, "teacher_head": teacher_head, "draft_head": draft_head}


def block_terms(teach_rows, draft_rows, teacher_head, draft_head):
    teach_logits = jnp.dot(teach_rows, teacher_head, preferred_element_type=jnp.float32)
    draft_logits = jnp.dot(draft_rows, draft_head, preferred_element_type=jnp.float32)
    teach_max = jnp.max(teach_logits, axis=1)
    draft_max = jnp.max(draft_logits, axis=1)
    teach_exp = jnp.exp(teach_logits - teach_max[:, None])
    draft_exp = jnp.exp(draft_logits - draft_max[:, None])
    teach_total = jnp.sum(teach_exp, axis=1)
    draft_total = jnp.sum(draft_exp, axis=1)
    cross_total = jnp.sum(teach_exp * (teach_logits - draft_logits), axis=1)
    token_kl = cross_total / teach_total - (teach_max + jnp.log(teach_total)) + (draft_max + jnp.log(draft_total))
    prob_gap = (draft_exp / draft_total[:, None] - teach_exp / teach_total[:, None]).astype(jnp.bfloat16)
    return token_kl, prob_gap


def reference(teacher_hidden, draft_hidden, teacher_head, draft_head):
    block = math.gcd(TOKENS, 256)
    count = TOKENS // block
    teach_blocks = teacher_hidden.reshape(count, block, D)
    draft_blocks = draft_hidden.reshape(count, block, DD)

    def step(carry, pieces):
        teach_rows, draft_rows = pieces
        token_kl, prob_gap = block_terms(teach_rows, draft_rows, teacher_head, draft_head)
        carry = carry + jnp.dot(draft_rows.T, prob_gap, preferred_element_type=jnp.float32)
        return carry, token_kl

    start = jnp.zeros((DD, VOCAB), jnp.float32)
    grad_sum, kl_blocks = lax.scan(step, start, (teach_blocks, draft_blocks))
    return kl_blocks.reshape(TOKENS), grad_sum.astype(jnp.bfloat16)
```

```python
import jax
import jax.numpy as jnp
from jax import lax
from jax.sharding import PartitionSpec as P


def merge(stats, axis):
    every = lax.all_gather(stats, axis)
    teach_max = jnp.max(every[:, 0], axis=0)
    draft_max = jnp.max(every[:, 1], axis=0)
    teach_scale = jnp.exp(every[:, 0] - teach_max)
    draft_scale = jnp.exp(every[:, 1] - draft_max)
    return jnp.stack([
        teach_max,
        draft_max,
        jnp.sum(every[:, 2] * teach_scale, axis=0),
        jnp.sum(every[:, 3] * teach_scale, axis=0),
        jnp.sum(every[:, 4] * draft_scale, axis=0),
    ])


def local(teacher_hidden, draft_hidden, teacher_head, draft_head):
    teacher_width = teacher_hidden.shape[1]
    own_rows = teacher_hidden.shape[0]
    joined = jnp.concatenate([teacher_hidden, draft_hidden], axis=1)
    gathered = lax.all_gather(joined, "context", axis=0, tiled=True)
    draft_rows = gathered[:, teacher_width:]
    teach_logits = jnp.dot(
        gathered[:, :teacher_width], teacher_head, preferred_element_type=jnp.float32
    )
    draft_logits = jnp.dot(draft_rows, draft_head, preferred_element_type=jnp.float32)
    teach_peak = jnp.max(teach_logits, axis=1)
    draft_peak = jnp.max(draft_logits, axis=1)
    teach_exp = jnp.exp(teach_logits - teach_peak[:, None])
    draft_exp = jnp.exp(draft_logits - draft_peak[:, None])
    stats = jnp.stack([
        teach_peak,
        draft_peak,
        jnp.sum(teach_exp, axis=1),
        jnp.sum(teach_exp * (teach_logits - draft_logits), axis=1),
        jnp.sum(draft_exp, axis=1),
    ])
    teach_max, draft_max, teach_total, cross_total, draft_total = merge(
        merge(stats, "context"), "tensor"
    )
    kl_rows = (
        cross_total / teach_total
        - (teach_max + jnp.log(teach_total))
        + (draft_max + jnp.log(draft_total))
    )
    token_kl = lax.dynamic_slice_in_dim(kl_rows, lax.axis_index("context") * own_rows, own_rows, 0)
    draft_factor = jnp.exp(draft_peak - draft_max) / draft_total
    teach_factor = jnp.exp(teach_peak - teach_max) / teach_total
    prob_gap = (draft_exp * draft_factor[:, None] - teach_exp * teach_factor[:, None]).astype(
        jnp.bfloat16
    )
    local_grad = jnp.dot(draft_rows.T, prob_gap, preferred_element_type=jnp.float32)
    head_grad = lax.psum_scatter(local_grad, "dp", scatter_dimension=0, tiled=True)
    return (token_kl, head_grad.astype(jnp.bfloat16))


def solution(mesh):
    in_specs = (
        P(("dp", "context"), None),
        P(("dp", "context"), None),
        P(None, ("tensor", "context")),
        P(None, ("tensor", "context")),
    )
    out_specs = (P(("dp", "context")), P("dp", ("tensor", "context")))
    return jax.shard_map(local, mesh=mesh, in_specs=in_specs, out_specs=out_specs, check_vma=False)
```

```python
import functools

import jax
import jax.numpy as jnp
from jax import lax
from jax.experimental import pallas as pl
from jax.experimental.pallas import tpu as pltpu
from jax.sharding import PartitionSpec as P

MESH = pl.DeviceIdType.MESH
F32 = jnp.float32
BF16 = jnp.bfloat16
SIDE = 4
PLANE = SIDE * SIDE
RUN = 16


def wrap(value, size):
    return lax.rem(value + size, size)


class Spread:
    def __init__(self, place, width, send, recv, number, where):
        core, z, y, x = where
        self.core, self.z, self.send, self.recv, self.number = core, z, send, recv, number
        self.place, self.width = place, width
        self.axes = ((x, y), (y, x))

    def ref(self, half, first, second, part):
        slot = second * SIDE + first if half == 0 else first * SIDE + second
        columns = self.width // 2
        start = half * columns
        if part is None:
            return self.place(slot, start, columns)
        return self.place(slot, start + part * (columns // 2), columns // 2)

    def target(self, half, step_first, step_second):
        first, second = self.axes[half]
        first, second = wrap(first + step_first, SIDE), wrap(second + step_second, SIDE)
        context = second * SIDE + first if half == 0 else first * SIDE + second
        return (self.core, self.z, context)

    def plan(self, half, number):
        if number < 2:
            way = (1, -1)[number]
            return (0, 0), None, (way, 0)
        if number < 4:
            way = (1, -1)[number - 2]
            return (-way, 0), number - 2, (way, 0)
        offset = (0, -1, 1, 2)[(number - 4) // 4]
        kind = (number - 4) % 4
        way = (1, -1)[kind % 2]
        if kind < 2:
            return (offset, 0), None, (0, way)
        return (offset, -way), kind % 2, (0, way)

    def copy(self, half, number, incoming=False):
        slot, part, steps = self.plan(half, number)
        first, second = self.axes[half]
        if incoming:
            slot = (slot[0] - steps[0], slot[1] - steps[1])
        ref = self.ref(half, wrap(first + slot[0], SIDE), wrap(second + slot[1], SIDE), part)
        return pltpu.make_async_remote_copy(
            src_ref=ref, dst_ref=ref,
            send_sem=self.send.at[self.number, half, number], recv_sem=self.recv.at[self.number, half, number],
            device_id=self.target(half, *steps), device_id_type=MESH,
        )

    def start(self, *numbers):
        for number in numbers:
            for half in range(2):
                self.copy(half, number).start()

    def arrived(self, *numbers):
        for number in numbers:
            for half in range(2):
                self.copy(half, number, incoming=True).wait_recv()

    def begin(self):
        self.start(0, 1, 4, 5)

    def second(self):
        self.arrived(0)
        self.start(2, 8, 9)
        self.arrived(1)
        self.start(3, 12, 13)
        self.arrived(4)
        self.start(6)
        self.arrived(5)
        self.start(7)

    def third(self):
        self.arrived(2, 3)
        self.start(16, 17)
        for number in (8, 9, 12, 13):
            self.arrived(number)
            self.start(number + 2)

    def fourth(self):
        self.arrived(16)
        self.start(18)
        self.arrived(17)
        self.start(19)

    def finish(self):
        self.arrived(6, 7, 10, 11, 14, 15, 18, 19)

    def sent(self):
        for number in range(20):
            for half in range(2):
                self.copy(half, number).wait_send()


def kernel(depth, teach_ref, draft_ref, teach_head_ref, draft_head_ref, kl_ref, grad_ref, rows, heads, extra, mate_rows,
           teach_exp, draft_exp, table, plane_stats, depth_stats, total_stats, gap_own, gap_out, gap_mate, gap_in,
           kl_own, kl_in, total, load_sem, spread_send, spread_recv, head_send, head_recv, mate_send, mate_recv,
           piece_send, piece_recv, plane_send, plane_recv, depth_send, depth_recv, gap_send, gap_recv, kl_send, kl_recv):
    teach_width = teach_ref.shape[1]
    draft_width = draft_ref.shape[1]
    width = teach_width + draft_width
    part = draft_width // 2
    vocab = teach_head_ref.shape[1]
    half_vocab = vocab // 2
    count = PLANE * RUN
    core = lax.axis_index("dp")
    z = lax.axis_index("tensor")
    context = lax.axis_index("context")
    y, x = context // SIDE, lax.rem(context, SIDE)
    other = 1 - core
    sequence = lax.rem(z, 2)
    above, below = wrap(z + 1, depth), wrap(z - 1, depth)
    mate = (other, z, context)
    here = pl.ds(pl.multiple_of(context * RUN, RUN), RUN)

    loads = [
        pltpu.make_async_copy(teach_head_ref, heads.at[0, pl.ds(0, teach_width)], load_sem.at[0]),
        pltpu.make_async_copy(draft_head_ref, heads.at[0, pl.ds(teach_width, draft_width)], load_sem.at[1]),
    ]

    def piece(index, group, to_mate):
        owner = other if to_mate else core
        from_rows = pl.ds(pl.multiple_of(owner * 2 * RUN + group * RUN, RUN), RUN)
        source, columns = (
            (teach_ref, pl.ds(0, teach_width)), (draft_ref, pl.ds(teach_width, draft_width))
        )[index]
        return source.at[from_rows], rows.at[group, here, columns], 2 * group + index

    def extra_piece(to_mate):
        owner = other if to_mate else core
        return draft_ref.at[:, pl.ds(pl.multiple_of(owner * part, part), part)], extra.at[context], 4

    def local_copy(source, target, number):
        return pltpu.make_async_copy(source, target, load_sem.at[2 + number])

    def mate_copy(source, target, number):
        return pltpu.make_async_remote_copy(
            src_ref=source, dst_ref=target, send_sem=piece_send.at[number], recv_sem=piece_recv.at[number],
            device_id=mate, device_id_type=MESH,
        )

    pieces = [(index, group) for group in range(2) for index in range(2)]
    holds_rows = core == sequence

    @pl.when(holds_rows)
    def _():
        for index, group in pieces:
            local_copy(*piece(index, group, False)).start()

    @pl.when(jnp.logical_not(holds_rows))
    def _():
        local_copy(*extra_piece(False)).start()

    for load in loads:
        load.start()

    barrier = pltpu.get_barrier_semaphore()
    partners = [mate] + [(c, level, context) for c in (core, other) for level in (above, below)]
    partners += [(core, z, wrap(context + step, PLANE)) for step in range(1, PLANE)]
    partners += [(core, wrap(z + step, depth), context) for step in range(2, depth, 2)]
    for partner in partners:
        pl.semaphore_signal(barrier, inc=1, device_id=partner, device_id_type=MESH)
    pl.semaphore_wait(barrier, len(partners))

    @pl.when(holds_rows)
    def _():
        for index, group in pieces:
            mate_copy(*piece(index, group, True)).start()

    @pl.when(jnp.logical_not(holds_rows))
    def _():
        mate_copy(*extra_piece(True)).start()

    where = (core, z, y, x)

    def group_place(group):
        return lambda slot, start, columns: rows.at[
            group, pl.ds(pl.multiple_of(slot * RUN, RUN), RUN), pl.ds(start, columns)]

    first = Spread(group_place(0), width, spread_send, spread_recv, 0, where)
    second = Spread(group_place(1), width, spread_send, spread_recv, 1, where)
    third = Spread(lambda slot, start, columns: extra.at[slot, :, pl.ds(start, columns)], part, spread_send, spread_recv,
                   2, where)

    @pl.when(holds_rows)
    def _():
        for index, group in pieces:
            local_copy(*piece(index, group, False)).wait()

    @pl.when(jnp.logical_not(holds_rows))
    def _():
        for index, group in pieces:
            mate_copy(*piece(index, group, True)).wait_recv()

    first.begin()
    for load in loads:
        load.wait()

    def head_copy(side, stage):
        depth_rows = width // 2
        half_rows = pl.ds(pl.multiple_of(core * depth_rows, depth_rows), depth_rows)
        columns = pl.ds(side * half_vocab, half_vocab)
        source = heads.at[0 if stage == 0 else 1, half_rows, columns]
        target = (core, (below, above)[side], context) if stage == 0 else mate
        return pltpu.make_async_remote_copy(
            src_ref=source, dst_ref=heads.at[1, half_rows, columns], send_sem=head_send.at[stage, side],
            recv_sem=head_recv.at[stage, side], device_id=target, device_id_type=MESH,
        )

    for side in range(2):
        head_copy(side, 0).start()

    first.second()
    first.third()
    second.begin()
    first.fourth()
    first.finish()

    def share_rows(group):
        return pltpu.make_async_remote_copy(
            src_ref=rows.at[group, :, pl.ds(pl.multiple_of(teach_width + other * part, part), part)],
            dst_ref=mate_rows.at[group], send_sem=mate_send.at[group], recv_sem=mate_recv.at[group],
            device_id=mate, device_id_type=MESH,
        )

    def logits(group, which):
        columns = pl.ds(which * vocab, vocab)
        teach_exp[group, :, columns] = jnp.dot(
            rows[group, :, :teach_width], heads[which, :teach_width, :], preferred_element_type=F32)
        draft_exp[group, :, columns] = jnp.dot(
            rows[group, :, teach_width:], heads[which, teach_width:, :], preferred_element_type=F32)

    block = 32

    def statistics(group):
        @pl.loop(0, count // block)
        def _(step):
            some = pl.ds(pl.multiple_of(step * block, block), block)
            teach = teach_exp[group, some, :]
            draft = draft_exp[group, some, :]
            teach_max = jnp.max(teach, axis=1, keepdims=True)
            draft_max = jnp.max(draft, axis=1, keepdims=True)
            teach_e = jnp.exp(teach - teach_max)
            draft_e = jnp.exp(draft - draft_max)
            teach_sum = jnp.sum(teach_e, axis=1, keepdims=True)
            cross_sum = jnp.sum(teach_e * (teach - draft), axis=1, keepdims=True)
            draft_sum = jnp.sum(draft_e, axis=1, keepdims=True)
            teach_exp[group, some, :] = teach_e
            draft_exp[group, some, :] = draft_e
            lane = lax.broadcasted_iota(jnp.int32, (block, 128), 1)
            wide = jnp.zeros((block, 128), F32)
            for position, value in ((0, teach_max), (1, teach_max), (2, draft_max), (4, teach_sum), (5, cross_sum),
                                    (6, draft_sum)):
                wide = jnp.where(lane == position, value, wide)
            table[some, :] = wide

        plane_stats[group, context] = jnp.transpose(table[...])[:8]

    def plane_copy(group, step, incoming=False):
        slot = wrap(context - step, PLANE) if incoming else context
        return pltpu.make_async_remote_copy(
            src_ref=plane_stats.at[group, slot], dst_ref=plane_stats.at[group, slot],
            send_sem=plane_send.at[group, step], recv_sem=plane_recv.at[group, step],
            device_id=(core, z, wrap(context + step, PLANE)), device_id_type=MESH,
        )

    level = z // 2
    levels = depth // 2

    def depth_copy(group, step, incoming=False):
        slot = wrap(level - step, levels) if incoming else level
        return pltpu.make_async_remote_copy(
            src_ref=depth_stats.at[group, slot], dst_ref=depth_stats.at[group, slot],
            send_sem=depth_send.at[group, step], recv_sem=depth_recv.at[group, step],
            device_id=(core, wrap(z + 2 * step, depth), context), device_id_type=MESH,
        )

    def merge(ref, group, members):
        peak = ref[group, 0, 0:4, :]
        for member in range(1, members):
            peak = jnp.maximum(peak, ref[group, member, 0:4, :])
        summed = jnp.zeros_like(peak)
        for member in range(members):
            summed += ref[group, member, 4:8, :] * jnp.exp(ref[group, member, 0:4, :] - peak)
        return peak, summed

    def send_plane(group):
        for step in range(1, PLANE):
            plane_copy(group, step).start()

    def send_depth(group):
        for step in range(1, PLANE):
            plane_copy(group, step, incoming=True).wait_recv()
        peak, summed = merge(plane_stats, group, PLANE)
        depth_stats[group, level, 0:4, :] = peak
        depth_stats[group, level, 4:8, :] = summed
        for step in range(1, levels):
            depth_copy(group, step).start()

    def gap_copy(group, number, incoming=False):
        if number == 0:
            source, target, device = gap_own.at[group], gap_mate.at[group], mate
        else:
            side, swap = (number - 1) // 2, (number - 1) % 2
            source = gap_out.at[group, side]
            owner = (other if swap else core) if incoming else core
            target = gap_in.at[owner * 2 + group, side]
            device = (other if swap else core, (above, below)[side], context)
        return pltpu.make_async_remote_copy(
            src_ref=source, dst_ref=target, send_sem=gap_send.at[group, number], recv_sem=gap_recv.at[group, number],
            device_id=device, device_id_type=MESH,
        )

    def gaps(group):
        for step in range(1, levels):
            depth_copy(group, step, incoming=True).wait_recv()
        peak, summed = merge(depth_stats, group, levels)
        teach_max, draft_max = peak[0:1], peak[2:3]
        teach_total, cross_total, draft_total = summed[0:1], summed[1:2], summed[2:3]
        token_kl = cross_total / teach_total - (teach_max + jnp.log(teach_total)) + (draft_max + jnp.log(draft_total))
        kl_own[group] = jnp.broadcast_to(token_kl, (8, count))
        mine = plane_stats[group, context]
        total_stats[...] = jnp.zeros_like(total_stats)
        total_stats[0:1, :] = jnp.exp(mine[0:1] - teach_max) / teach_total
        total_stats[1:2, :] = jnp.exp(mine[2:3] - draft_max) / draft_total
        table[...] = jnp.transpose(total_stats[...])

        @pl.loop(0, count // block)
        def _(step):
            some = pl.ds(pl.multiple_of(step * block, block), block)
            factors = table[some, :]
            gap = (draft_exp[group, some, :] * factors[:, 1:2] - teach_exp[group, some, :] * factors[:, 0:1]).astype(BF16)
            gap_own[group, some, :] = gap[:, :vocab]
            gap_out[group, 0, some, :] = gap[:, vocab:vocab + half_vocab]
            gap_out[group, 1, some, :] = gap[:, vocab + half_vocab:]

        for number in (1, 2, 3, 4, 0):
            gap_copy(group, number).start()

    contract = (((0,), (0,)), ((), ()))

    def add(left, right, columns=slice(None), fresh=False):
        product = lax.dot_general(left, right, contract, preferred_element_type=F32)
        if fresh:
            total[:, columns] = product
        else:
            total[:, columns] += product

    def own_grad(group):
        mine = rows[group, :, pl.ds(pl.multiple_of(teach_width + core * part, part), part)]
        add(mine, gap_own[group], fresh=group == 0)

    def mate_grad(group):
        gap_copy(group, 0).wait_recv()
        add(mate_rows[group], gap_mate[group])

    def extra_grad(group):
        for number in range(1, 5):
            gap_copy(group, number, incoming=True).wait_recv()
        for owner in range(2):
            start = (owner * 2 + group) * RUN
            left = extra[:, start:start + RUN, :].reshape(count, part)
            for side in range(2):
                add(left, gap_in[owner * 2 + group, side], slice(side * half_vocab, (side + 1) * half_vocab))

    second.second()
    share_rows(0).start()
    for side in range(2):
        head_copy(side, 0).wait_recv()
        head_copy(side, 1).start()
    logits(0, 0)
    second.third()

    @pl.when(holds_rows)
    def _():
        mate_copy(*extra_piece(True)).wait_recv()

    @pl.when(jnp.logical_not(holds_rows))
    def _():
        local_copy(*extra_piece(False)).wait()

    third.begin()
    for side in range(2):
        pltpu.make_async_remote_copy(
            src_ref=heads.at[1, pl.ds(pl.multiple_of(other * (width // 2), width // 2), width // 2),
                             pl.ds(side * half_vocab, half_vocab)],
            dst_ref=heads.at[1, pl.ds(pl.multiple_of(other * (width // 2), width // 2), width // 2),
                             pl.ds(side * half_vocab, half_vocab)],
            send_sem=head_send.at[1, side], recv_sem=head_recv.at[1, side], device_id=mate, device_id_type=MESH,
        ).wait_recv()
    logits(0, 1)
    statistics(0)
    send_plane(0)
    second.fourth()
    send_depth(0)
    second.finish()
    share_rows(1).start()
    logits(1, 0)
    logits(1, 1)
    statistics(1)
    send_plane(1)
    third.second()
    gaps(0)
    send_depth(1)
    third.third()
    own_grad(0)
    share_rows(0).wait_recv()
    mate_grad(0)
    third.fourth()
    third.finish()
    extra_grad(0)
    gaps(1)

    def kl_copy(number, source_core):
        device = (sequence, (z, below)[number], context)
        return pltpu.make_async_remote_copy(
            src_ref=kl_own, dst_ref=kl_in.at[source_core], send_sem=kl_send.at[number],
            recv_sem=kl_recv.at[number * 2 + source_core], device_id=device, device_id_type=MESH,
        )

    kl_copy(1, core).start()

    @pl.when(jnp.logical_not(holds_rows))
    def _():
        kl_copy(0, core).start()

    own_grad(1)
    share_rows(1).wait_recv()
    mate_grad(1)

    @pl.when(holds_rows)
    def _():
        kl_copy(0, other).wait_recv()
        kl_in[core] = kl_own[...]

    @pl.when(jnp.logical_not(holds_rows))
    def _():
        kl_copy(1, 0).wait_recv()
        kl_copy(1, 1).wait_recv()

    lane = lax.broadcasted_iota(jnp.int32, (8, count), 1)
    token_kl = jnp.zeros((8, count), F32)
    for owner in range(2):
        for group in range(2):
            start = (owner * 2 + group) * RUN
            moved = pltpu.roll(kl_in[owner, group], lax.rem(start - context * RUN + count, count), 1)
            token_kl = jnp.where((lane >= start) & (lane < start + RUN), moved, token_kl)
    kl_ref[...] = token_kl[0:1, 0:4 * RUN]

    extra_grad(1)
    grad_ref[...] = total[...].astype(grad_ref.dtype)

    first.sent()
    second.sent()
    third.sent()
    for side in range(2):
        head_copy(side, 0).wait_send()
        head_copy(side, 1).wait_send()

    @pl.when(holds_rows)
    def _():
        for index, group in pieces:
            mate_copy(*piece(index, group, True)).wait_send()

    @pl.when(jnp.logical_not(holds_rows))
    def _():
        mate_copy(*extra_piece(True)).wait_send()
        kl_copy(0, core).wait_send()

    kl_copy(1, core).wait_send()
    for group in range(2):
        share_rows(group).wait_send()
        for step in range(1, PLANE):
            plane_copy(group, step).wait_send()
        for step in range(1, levels):
            depth_copy(group, step).wait_send()
        for number in range(5):
            gap_copy(group, number).wait_send()


def local(depth, teacher_hidden, draft_hidden, teacher_head, draft_head):
    teach_width, vocab = teacher_head.shape
    draft_width = draft_head.shape[0]
    width, part = teach_width + draft_width, draft_width // 2
    count, levels = PLANE * RUN, depth // 2
    own_rows = teacher_hidden.shape[0]
    dma = pltpu.SemaphoreType.DMA
    scratch = [
        pltpu.VMEM((2, count, width), BF16),
        pltpu.VMEM((2, width, vocab), BF16),
        pltpu.VMEM((PLANE, own_rows, part), BF16),
        pltpu.VMEM((2, count, part), BF16),
        pltpu.VMEM((2, count, 2 * vocab), F32),
        pltpu.VMEM((2, count, 2 * vocab), F32),
        pltpu.VMEM((count, 128), F32),
        pltpu.VMEM((2, PLANE, 8, count), F32),
        pltpu.VMEM((2, levels, 8, count), F32),
        pltpu.VMEM((128, count), F32),
        pltpu.VMEM((2, count, vocab), BF16),
        pltpu.VMEM((2, 2, count, vocab // 2), BF16),
        pltpu.VMEM((2, count, vocab), BF16),
        pltpu.VMEM((4, 2, count, vocab // 2), BF16),
        pltpu.VMEM((2, 8, count), F32),
        pltpu.VMEM((2, 2, 8, count), F32),
        pltpu.VMEM((part, vocab), F32),
        dma((7,)),
        dma((3, 2, 20)), dma((3, 2, 20)),
        dma((2, 2)), dma((2, 2)),
        dma((2,)), dma((2,)),
        dma((5,)), dma((5,)),
        dma((2, PLANE)), dma((2, PLANE)),
        dma((2, levels)), dma((2, levels)),
        dma((2, 5)), dma((2, 5)),
        dma((2,)), dma((4,)),
    ]
    token_kl, head_grad = pl.pallas_call(
        functools.partial(kernel, depth),
        out_shape=(jax.ShapeDtypeStruct((1, own_rows), F32), jax.ShapeDtypeStruct((part, vocab), BF16)),
        in_specs=[pl.BlockSpec(memory_space=pl.ANY)] * 4,
        out_specs=(pl.BlockSpec(memory_space=pltpu.VMEM), pl.BlockSpec(memory_space=pltpu.VMEM)),
        scratch_shapes=scratch,
        compiler_params=pltpu.CompilerParams(collective_id=0, has_side_effects=True, vmem_limit_bytes=60 << 20),
        name="distill",
    )(teacher_hidden, draft_hidden, teacher_head, draft_head)
    return token_kl.reshape(own_rows), head_grad


def solution(mesh):
    in_specs = (
        P(("dp", "context"), None),
        P(("dp", "context"), None),
        P(None, ("tensor", "context")),
        P(None, ("tensor", "context")),
    )
    out_specs = (P(("dp", "context")), P("dp", ("tensor", "context")))
    return jax.shard_map(
        functools.partial(local, mesh.shape["tensor"]), mesh=mesh, in_specs=in_specs, out_specs=out_specs, check_vma=False
    )
```

```python
import functools

import jax
import jax.numpy as jnp
from jax import lax
from jax.experimental import pallas as pl
from jax.experimental.pallas import tpu as pltpu
from jax.sharding import PartitionSpec as P

MESH = pl.DeviceIdType.MESH
F32 = jnp.float32
BF16 = jnp.bfloat16
SIDE = 4
PLANE = SIDE * SIDE
RUN = 16


def wrap(value, size):
    return lax.rem(value + size, size)


class Spread:
    CLASS = {0: 0, 1: 1, 4: 2, 5: 3, 8: 4, 9: 5, 12: 6, 13: 7, 2: 8, 3: 8, 16: 9, 17: 10}

    def __init__(self, place, slots, width, send, recv, number, where):
        self.slots = slots
        core, z, y, x = where
        self.core, self.z, self.send, self.recv, self.number = core, z, send, recv, number
        self.place, self.width = place, width
        self.axes = ((x, y), (y, x))

    def ref(self, half, first, second, part):
        slot = second * SIDE + first if half == 0 else first * SIDE + second
        columns = self.width // 2
        start = half * columns
        if part is None:
            return self.place(slot, start, columns)
        return self.place(slot, start + part * (columns // 2), columns // 2)

    def target(self, half, step_first, step_second):
        first, second = self.axes[half]
        first, second = wrap(first + step_first, SIDE), wrap(second + step_second, SIDE)
        context = second * SIDE + first if half == 0 else first * SIDE + second
        return (self.core, self.z, context)

    def plan(self, half, number):
        if number < 2:
            way = (1, -1)[number]
            return (0, 0), None, (way, 0)
        if number < 4:
            way = (1, -1)[number - 2]
            return (-way, 0), number - 2, (way, 0)
        offset = (0, -1, 1, 2)[(number - 4) // 4]
        kind = (number - 4) % 4
        way = (1, -1)[kind % 2]
        if kind < 2:
            return (offset, 0), None, (0, way)
        return (offset, -way), kind % 2, (0, way)

    def copy(self, half, number):
        slot, part, steps = self.plan(half, number)
        first, second = self.axes[half]
        ref = self.ref(half, wrap(first + slot[0], SIDE), wrap(second + slot[1], SIDE), part)
        return pltpu.make_async_remote_copy(
            src_ref=ref, dst_ref=ref,
            send_sem=self.send.at[self.number], recv_sem=self.recv.at[self.number, self.CLASS.get(number, 11)],
            device_id=self.target(half, *steps), device_id_type=MESH,
        )

    def bulk(self, kind, slots):
        ref = self.slots(slots)
        return pltpu.make_async_remote_copy(
            src_ref=ref, dst_ref=ref, send_sem=self.send.at[self.number], recv_sem=self.recv.at[self.number, kind],
            device_id=self.target(0, 1, 0), device_id_type=MESH,
        )

    def start(self, *numbers):
        for number in numbers:
            for half in range(2):
                self.copy(half, number).start()

    def arrived(self, number):
        self.bulk(self.CLASS[number], 1).wait_recv()

    def begin(self):
        self.start(0, 1, 4, 5)

    def second(self):
        self.arrived(0)
        self.start(2, 8, 9)
        self.arrived(1)
        self.start(3, 12, 13)
        self.arrived(4)
        self.start(6)
        self.arrived(5)
        self.start(7)

    def third(self):
        self.arrived(2)
        self.start(16, 17)
        for number in (8, 9, 12, 13):
            self.arrived(number)
            self.start(number + 2)

    def fourth(self):
        self.arrived(16)
        self.start(18)
        self.arrived(17)
        self.start(19)

    def finish(self):
        self.bulk(11, 4).wait_recv()

    def sent(self):
        self.bulk(0, PLANE - 1).wait_send()


def kernel(depth, teach_ref, draft_ref, teach_head_ref, draft_head_ref, kl_ref, grad_ref, rows, heads, extra,
           extra_low, mate_rows,
           teach_exp, draft_exp, table, plane_stats, depth_stats, total_stats, gap_own, gap_out, gap_mate, gap_in,
           kl_own, kl_in, total, far_sem, load_sem, low_send, low_recv, spread_send, spread_recv, head_send, head_recv, mate_send, mate_recv,
           piece_send, piece_recv, plane_send, plane_recv, depth_send, depth_recv, gap_send, gap_recv, kl_send, kl_recv):
    teach_width = teach_ref.shape[1]
    draft_width = draft_ref.shape[1]
    width = teach_width + draft_width
    part = draft_width // 2
    vocab = teach_head_ref.shape[1]
    half_vocab = vocab // 2
    count = PLANE * RUN
    core = lax.axis_index("dp")
    z = lax.axis_index("tensor")
    context = lax.axis_index("context")
    y, x = context // SIDE, lax.rem(context, SIDE)
    other = 1 - core
    sequence = lax.rem(z, 2)
    above, below = wrap(z + 1, depth), wrap(z - 1, depth)
    mate = (other, z, context)
    here = pl.ds(pl.multiple_of(context * RUN, RUN), RUN)

    loads = [
        pltpu.make_async_copy(teach_head_ref, heads.at[0, pl.ds(0, teach_width)], load_sem.at[0]),
        pltpu.make_async_copy(draft_head_ref, heads.at[0, pl.ds(teach_width, draft_width)], load_sem.at[0]),
    ]

    def piece(index, group, owner):
        from_rows = pl.ds(pl.multiple_of(owner * 2 * RUN + group * RUN, RUN), RUN)
        source, columns = (
            (teach_ref, pl.ds(0, teach_width)), (draft_ref, pl.ds(teach_width, draft_width))
        )[index]
        return source.at[from_rows], rows.at[group, here, columns], group

    def extra_piece(index, owner):
        source = draft_ref.at[pl.ds(index * 2 * RUN + RUN, RUN), pl.ds(pl.multiple_of(owner * part, part), part)]
        return source, extra.at[context, pl.ds(index * RUN, RUN)], 2

    def local_copy(source, target, number):
        return pltpu.make_async_copy(source, target, load_sem.at[1 + number])

    def mate_copy(source, target, number):
        return pltpu.make_async_remote_copy(
            src_ref=source, dst_ref=target, send_sem=piece_send.at[0], recv_sem=piece_recv.at[number],
            device_id=mate, device_id_type=MESH,
        )

    pieces = [(index, group) for group in range(2) for index in range(2)]
    holds_rows = core == sequence
    group_rows = [rows.at[group, here, :] for group in range(2)]

    @pl.when(holds_rows)
    def _():
        for index, group in pieces:
            local_copy(*piece(index, group, core)).start()

    @pl.when(jnp.logical_not(holds_rows))
    def _():
        for index in range(2):
            local_copy(*extra_piece(index, core)).start()

    for load in loads:
        load.start()

    barrier = pltpu.get_barrier_semaphore()
    partners = [mate] + [(c, level, context) for c in (core, other) for level in (above, below)]
    partners += [(core, z, y * SIDE + wrap(x + step, SIDE)) for step in (1, -1)]
    partners += [(core, z, wrap(y + step, SIDE) * SIDE + x) for step in (1, -1)]
    for partner in partners:
        pl.semaphore_signal(barrier, inc=1, device_id=partner, device_id_type=MESH)
    pl.semaphore_wait(barrier, len(partners))

    @pl.when(holds_rows)
    def _():
        for index, group in pieces:
            mate_copy(*piece(index, group, other)).start()

    @pl.when(jnp.logical_not(holds_rows))
    def _():
        for index in range(2):
            mate_copy(*extra_piece(index, other)).start()

    where = (core, z, y, x)

    def group_place(group):
        return lambda slot, start, columns: rows.at[
            group, pl.ds(pl.multiple_of(slot * RUN, RUN), RUN), pl.ds(start, columns)]

    def group_slots(group):
        return lambda slots: rows.at[group, pl.ds(0, slots * RUN), :]

    first = Spread(group_place(0), group_slots(0), width, spread_send, spread_recv, 0, where)
    second = Spread(group_place(1), group_slots(1), width, spread_send, spread_recv, 1, where)
    third = Spread(lambda slot, start, columns: extra.at[slot, :, pl.ds(start, columns)],
                   lambda slots: extra.at[pl.ds(0, slots)], part, spread_send, spread_recv, 2, where)

    def rows_here(group):
        @pl.when(holds_rows)
        def _():
            local_copy(group_rows[group], group_rows[group], group).wait()

        @pl.when(jnp.logical_not(holds_rows))
        def _():
            mate_copy(group_rows[group], group_rows[group], group).wait_recv()

    def reach(number):
        step = 1 << number
        for level in (wrap(z + step, depth), wrap(z - step, depth)):
            pl.semaphore_signal(far_sem.at[number], inc=1, device_id=(core, level, context), device_id_type=MESH)
        pl.semaphore_wait(far_sem.at[number], 2)

    rows_here(0)
    first.begin()
    pltpu.make_async_copy(heads.at[0], heads.at[0], load_sem.at[0]).wait()

    def head_copy(side, stage):
        depth_rows = width // 2
        half_rows = pl.ds(pl.multiple_of(core * depth_rows, depth_rows), depth_rows)
        columns = pl.ds(side * half_vocab, half_vocab)
        source = heads.at[0 if stage == 0 else 1, half_rows, columns]
        target = (core, (below, above)[side], context) if stage == 0 else mate
        return pltpu.make_async_remote_copy(
            src_ref=source, dst_ref=heads.at[1, half_rows, columns], send_sem=head_send.at[0],
            recv_sem=head_recv.at[stage], device_id=target, device_id_type=MESH,
        )

    def heads_all(ref, stage):
        return pltpu.make_async_remote_copy(src_ref=ref, dst_ref=ref, send_sem=head_send.at[0], recv_sem=head_recv.at[stage],
                                            device_id=mate, device_id_type=MESH)

    for side in range(2):
        head_copy(side, 0).start()

    first.second()
    first.third()
    rows_here(1)
    second.begin()
    first.fourth()
    reach(0)
    first.finish()

    def low_copy(side, swap):
        half_count = count // 2
        some = pl.ds(side * half_count, half_count)
        goal = other if swap else core
        return pltpu.make_async_remote_copy(
            src_ref=rows.at[0, some, pl.ds(pl.multiple_of(teach_width + goal * part, part), part)],
            dst_ref=extra_low.at[core, some], send_sem=low_send.at[0], recv_sem=low_recv.at[0],
            device_id=(goal, (above, below)[side], context), device_id_type=MESH,
        )

    low_all = pltpu.make_async_remote_copy(
        src_ref=extra_low, dst_ref=extra_low, send_sem=low_send.at[0], recv_sem=low_recv.at[0],
        device_id=(core, above, context), device_id_type=MESH,
    )
    for side in range(2):
        for swap in range(2):
            low_copy(side, swap).start()

    def share_rows(group):
        return pltpu.make_async_remote_copy(
            src_ref=rows.at[group, :, pl.ds(pl.multiple_of(teach_width + other * part, part), part)],
            dst_ref=mate_rows.at[group], send_sem=mate_send.at[group], recv_sem=mate_recv.at[group],
            device_id=mate, device_id_type=MESH,
        )

    def logits(group, which):
        columns = pl.ds(which * vocab, vocab)
        teach_exp[group, :, columns] = jnp.dot(
            rows[group, :, :teach_width], heads[which, :teach_width, :], preferred_element_type=F32)
        draft_exp[group, :, columns] = jnp.dot(
            rows[group, :, teach_width:], heads[which, teach_width:, :], preferred_element_type=F32)

    block = 32

    def statistics(group):
        @pl.loop(0, count // block)
        def _(step):
            some = pl.ds(pl.multiple_of(step * block, block), block)
            teach = teach_exp[group, some, :]
            draft = draft_exp[group, some, :]
            teach_max = jnp.max(teach, axis=1, keepdims=True)
            draft_max = jnp.max(draft, axis=1, keepdims=True)
            teach_e = jnp.exp(teach - teach_max)
            draft_e = jnp.exp(draft - draft_max)
            teach_sum = jnp.sum(teach_e, axis=1, keepdims=True)
            cross_sum = jnp.sum(teach_e * (teach - draft), axis=1, keepdims=True)
            draft_sum = jnp.sum(draft_e, axis=1, keepdims=True)
            teach_exp[group, some, :] = teach_e
            draft_exp[group, some, :] = draft_e
            lane = lax.broadcasted_iota(jnp.int32, (block, 128), 1)
            wide = jnp.zeros((block, 128), F32)
            for position, value in ((0, teach_max), (1, teach_max), (2, draft_max), (4, teach_sum), (5, cross_sum),
                                    (6, draft_sum)):
                wide = jnp.where(lane == position, value, wide)
            table[some, :] = wide

        plane_stats[group, context] = jnp.transpose(table[...])[:8]

    def plane_copy(group, step, slots=None):
        ref = plane_stats.at[group, context if slots is None else pl.ds(0, slots)]
        return pltpu.make_async_remote_copy(
            src_ref=ref, dst_ref=ref, send_sem=plane_send.at[group], recv_sem=plane_recv.at[group],
            device_id=(core, z, wrap(context + step, PLANE)), device_id_type=MESH,
        )

    level = z // 2
    levels = depth // 2

    def depth_copy(group, step, slots=None):
        ref = depth_stats.at[group, level if slots is None else pl.ds(0, slots)]
        return pltpu.make_async_remote_copy(
            src_ref=ref, dst_ref=ref, send_sem=depth_send.at[group], recv_sem=depth_recv.at[group],
            device_id=(core, wrap(z + 2 * step, depth), context), device_id_type=MESH,
        )

    def merge(ref, group, members):
        peak = ref[group, 0, 0:4, :]
        for member in range(1, members):
            peak = jnp.maximum(peak, ref[group, member, 0:4, :])
        summed = jnp.zeros_like(peak)
        for member in range(members):
            summed += ref[group, member, 4:8, :] * jnp.exp(ref[group, member, 0:4, :] - peak)
        return peak, summed

    def send_plane(group):
        for step in range(1, PLANE):
            plane_copy(group, step).start()

    def send_depth(group):
        plane_copy(group, 1, PLANE - 1).wait_recv()
        peak, summed = merge(plane_stats, group, PLANE)
        depth_stats[group, level, 0:4, :] = peak
        depth_stats[group, level, 4:8, :] = summed
        for step in range(1, levels):
            depth_copy(group, step).start()

    def gap_copy(group, number):
        if number == 0:
            source, target, device = gap_own.at[group], gap_mate.at[group], mate
        else:
            side, swap = (number - 1) // 2, (number - 1) % 2
            source, target = gap_out.at[group, side], gap_in.at[core * 2 + group, side]
            device = (other if swap else core, (above, below)[side], context)
        return pltpu.make_async_remote_copy(
            src_ref=source, dst_ref=target, send_sem=gap_send.at[group], recv_sem=gap_recv.at[group, min(number, 1)],
            device_id=device, device_id_type=MESH,
        )

    def gap_all(group, blocks):
        ref = gap_in.at[pl.ds(0, blocks)]
        return pltpu.make_async_remote_copy(
            src_ref=ref, dst_ref=ref, send_sem=gap_send.at[group], recv_sem=gap_recv.at[group, 1],
            device_id=mate, device_id_type=MESH,
        )

    def gaps(group):
        depth_copy(group, 1, levels - 1).wait_recv()
        peak, summed = merge(depth_stats, group, levels)
        teach_max, draft_max = peak[0:1], peak[2:3]
        teach_total, cross_total, draft_total = summed[0:1], summed[1:2], summed[2:3]
        token_kl = cross_total / teach_total - (teach_max + jnp.log(teach_total)) + (draft_max + jnp.log(draft_total))
        kl_own[group] = jnp.broadcast_to(token_kl, (8, count))
        mine = plane_stats[group, context]
        total_stats[...] = jnp.zeros_like(total_stats)
        total_stats[0:1, :] = jnp.exp(mine[0:1] - teach_max) / teach_total
        total_stats[1:2, :] = jnp.exp(mine[2:3] - draft_max) / draft_total
        table[...] = jnp.transpose(total_stats[...])

        @pl.loop(0, count // block)
        def _(step):
            some = pl.ds(pl.multiple_of(step * block, block), block)
            factors = table[some, :]
            gap = (draft_exp[group, some, :] * factors[:, 1:2] - teach_exp[group, some, :] * factors[:, 0:1]).astype(BF16)
            gap_own[group, some, :] = gap[:, :vocab]
            gap_out[group, 0, some, :] = gap[:, vocab:vocab + half_vocab]
            gap_out[group, 1, some, :] = gap[:, vocab + half_vocab:]

        for number in (1, 2, 3, 4, 0):
            gap_copy(group, number).start()

    contract = (((0,), (0,)), ((), ()))

    def add(left, right, columns=slice(None), fresh=False):
        product = lax.dot_general(left, right, contract, preferred_element_type=F32)
        if fresh:
            total[:, columns] = product
        else:
            total[:, columns] += product

    def own_grad(group):
        mine = rows[group, :, pl.ds(pl.multiple_of(teach_width + core * part, part), part)]
        add(mine, gap_own[group], fresh=group == 0)

    def mate_grad(group):
        gap_copy(group, 0).wait_recv()
        add(mate_rows[group], gap_mate[group])

    def extra_grad(group):
        gap_all(group, 2).wait_recv()
        for owner in range(2):
            if group == 0:
                left = extra_low[owner]
            else:
                left = extra[:, owner * RUN:(owner + 1) * RUN, :].reshape(count, part)
            for side in range(2):
                add(left, gap_in[owner * 2 + group, side], slice(side * half_vocab, (side + 1) * half_vocab))

    second.second()
    share_rows(0).start()
    reach(1)
    heads_all(heads.at[1, pl.ds(0, width // 2)], 0).wait_recv()
    for side in range(2):
        head_copy(side, 1).start()
    logits(0, 0)
    second.third()

    @pl.when(holds_rows)
    def _():
        mate_copy(extra.at[context], extra.at[context], 2).wait_recv()

    @pl.when(jnp.logical_not(holds_rows))
    def _():
        local_copy(extra.at[context], extra.at[context], 2).wait()

    third.begin()
    reach(2)
    heads_all(heads.at[1, pl.ds(0, width // 2)], 1).wait_recv()
    logits(0, 1)
    statistics(0)
    send_plane(0)
    second.fourth()
    send_depth(0)
    second.finish()
    share_rows(1).start()
    logits(1, 0)
    logits(1, 1)
    statistics(1)
    send_plane(1)
    third.second()
    gaps(0)
    send_depth(1)
    third.third()
    own_grad(0)
    share_rows(0).wait_recv()
    mate_grad(0)
    third.fourth()
    third.finish()
    low_all.wait_recv()
    extra_grad(0)
    gaps(1)

    def kl_copy(number, source_core):
        device = (sequence, (z, below)[number], context)
        return pltpu.make_async_remote_copy(
            src_ref=kl_own, dst_ref=kl_in.at[source_core], send_sem=kl_send.at[number],
            recv_sem=kl_recv.at[number], device_id=device, device_id_type=MESH,
        )

    kl_copy(1, core).start()

    @pl.when(jnp.logical_not(holds_rows))
    def _():
        kl_copy(0, core).start()

    own_grad(1)
    share_rows(1).wait_recv()
    mate_grad(1)

    @pl.when(holds_rows)
    def _():
        kl_copy(0, other).wait_recv()
        kl_in[core] = kl_own[...]

    @pl.when(jnp.logical_not(holds_rows))
    def _():
        pltpu.make_async_remote_copy(
            src_ref=kl_in, dst_ref=kl_in, send_sem=kl_send.at[1], recv_sem=kl_recv.at[1],
            device_id=mate, device_id_type=MESH,
        ).wait_recv()

    lane = lax.broadcasted_iota(jnp.int32, (8, count), 1)
    token_kl = jnp.zeros((8, count), F32)
    for owner in range(2):
        for group in range(2):
            start = (owner * 2 + group) * RUN
            moved = pltpu.roll(kl_in[owner, group], lax.rem(start - context * RUN + count, count), 1)
            token_kl = jnp.where((lane >= start) & (lane < start + RUN), moved, token_kl)
    kl_ref[...] = token_kl[0:1, 0:4 * RUN]

    extra_grad(1)
    grad_ref[...] = total[...].astype(grad_ref.dtype)

    first.sent()
    second.sent()
    third.sent()
    low_all.wait_send()
    heads_all(heads.at[1], 0).wait_send()

    @pl.when(holds_rows)
    def _():
        two = rows.at[0, pl.ds(0, 2 * RUN), :]
        mate_copy(two, two, 0).wait_send()

    @pl.when(jnp.logical_not(holds_rows))
    def _():
        mate_copy(extra.at[context], extra.at[context], 2).wait_send()
        kl_copy(0, core).wait_send()

    kl_copy(1, core).wait_send()
    for group in range(2):
        share_rows(group).wait_send()
        plane_copy(group, 1, PLANE - 1).wait_send()
        depth_copy(group, 1, levels - 1).wait_send()
        gap_all(group, 3).wait_send()


def settle(kl_ref, grad_ref, kl_out, grad_out):
    kl_out[...] = kl_ref[...]
    grad_out[...] = grad_ref[...]


def local(depth, teacher_hidden, draft_hidden, teacher_head, draft_head):
    teach_width, vocab = teacher_head.shape
    draft_width = draft_head.shape[0]
    width, part = teach_width + draft_width, draft_width // 2
    count, levels = PLANE * RUN, depth // 2
    own_rows = teacher_hidden.shape[0]
    dma = pltpu.SemaphoreType.DMA
    scratch = [
        pltpu.VMEM((2, count, width), BF16),
        pltpu.VMEM((2, width, vocab), BF16),
        pltpu.VMEM((PLANE, own_rows // 2, part), BF16),
        pltpu.VMEM((2, count, part), BF16),
        pltpu.VMEM((2, count, part), BF16),
        pltpu.VMEM((2, count, 2 * vocab), F32),
        pltpu.VMEM((2, count, 2 * vocab), F32),
        pltpu.VMEM((count, 128), F32),
        pltpu.VMEM((2, PLANE, 8, count), F32),
        pltpu.VMEM((2, levels, 8, count), F32),
        pltpu.VMEM((128, count), F32),
        pltpu.VMEM((2, count, vocab), BF16),
        pltpu.VMEM((2, 2, count, vocab // 2), BF16),
        pltpu.VMEM((2, count, vocab), BF16),
        pltpu.VMEM((4, 2, count, vocab // 2), BF16),
        pltpu.VMEM((2, 8, count), F32),
        pltpu.VMEM((2, 2, 8, count), F32),
        pltpu.VMEM((part, vocab), F32),
        pltpu.SemaphoreType.REGULAR((3,)),
        dma((4,)),
        dma((1,)), dma((1,)),
        dma((3,)), dma((3, 12)),
        dma((1,)), dma((2,)),
        dma((2,)), dma((2,)),
        dma((1,)), dma((3,)),
        dma((2,)), dma((2,)),
        dma((2,)), dma((2,)),
        dma((2,)), dma((2, 2)),
        dma((2,)), dma((2,)),
    ]
    token_kl, head_grad = pl.pallas_call(
        functools.partial(kernel, depth),
        out_shape=(jax.ShapeDtypeStruct((1, own_rows), F32), jax.ShapeDtypeStruct((part, vocab), BF16)),
        in_specs=[pl.BlockSpec(memory_space=pl.ANY)] * 4,
        out_specs=(pl.BlockSpec(memory_space=pltpu.VMEM), pl.BlockSpec(memory_space=pltpu.VMEM)),
        scratch_shapes=scratch,
        compiler_params=pltpu.CompilerParams(collective_id=0, has_side_effects=True, vmem_limit_bytes=60 << 20),
        name="distill",
    )(teacher_hidden, draft_hidden, teacher_head, draft_head)
    token_kl, head_grad = pl.pallas_call(
        settle,
        out_shape=(jax.ShapeDtypeStruct((1, own_rows), F32), jax.ShapeDtypeStruct((part, vocab), BF16)),
        in_specs=[pl.BlockSpec(memory_space=pltpu.VMEM)] * 2,
        out_specs=(pl.BlockSpec(memory_space=pltpu.VMEM), pl.BlockSpec(memory_space=pltpu.VMEM)),
        name="settle",
    )(token_kl, head_grad)
    return token_kl.reshape(own_rows), head_grad


def solution(mesh):
    in_specs = (
        P(("dp", "context"), None),
        P(("dp", "context"), None),
        P(None, ("tensor", "context")),
        P(None, ("tensor", "context")),
    )
    out_specs = (P(("dp", "context")), P("dp", ("tensor", "context")))
    return jax.shard_map(
        functools.partial(local, mesh.shape["tensor"]), mesh=mesh, in_specs=in_specs, out_specs=out_specs, check_vma=False
    )
```

```python
import functools

import jax
import jax.numpy as jnp
from jax import lax
from jax.experimental import pallas as pl
from jax.experimental.pallas import tpu as pltpu
from jax.sharding import PartitionSpec as P

MESH = pl.DeviceIdType.MESH
F32 = jnp.float32
BF16 = jnp.bfloat16
SIDE = 4
PLANE = SIDE * SIDE
RUN = 16


def wrap(value, size):
    return lax.rem(value + size, size)


class Spread:
    CLASS = {0: 0, 1: 1, 4: 2, 5: 3, 8: 4, 9: 5, 12: 6, 13: 7, 2: 8, 3: 8, 16: 9, 17: 10}

    def __init__(self, place, slots, width, send, recv, number, where):
        self.slots = slots
        core, z, y, x = where
        self.core, self.z, self.send, self.recv, self.number = core, z, send, recv, number
        self.place, self.width = place, width
        self.axes = ((x, y), (y, x))

    def ref(self, half, first, second, part):
        slot = second * SIDE + first if half == 0 else first * SIDE + second
        columns = self.width // 2
        start = half * columns
        if part is None:
            return self.place(slot, start, columns)
        return self.place(slot, start + part * (columns // 2), columns // 2)

    def target(self, half, step_first, step_second):
        first, second = self.axes[half]
        first, second = wrap(first + step_first, SIDE), wrap(second + step_second, SIDE)
        context = second * SIDE + first if half == 0 else first * SIDE + second
        return (self.core, self.z, context)

    def plan(self, half, number):
        if number < 2:
            way = (1, -1)[number]
            return (0, 0), None, (way, 0)
        if number < 4:
            way = (1, -1)[number - 2]
            return (-way, 0), number - 2, (way, 0)
        offset = (0, -1, 1, 2)[(number - 4) // 4]
        kind = (number - 4) % 4
        way = (1, -1)[kind % 2]
        if kind < 2:
            return (offset, 0), None, (0, way)
        return (offset, -way), kind % 2, (0, way)

    def copy(self, half, number):
        slot, part, steps = self.plan(half, number)
        first, second = self.axes[half]
        ref = self.ref(half, wrap(first + slot[0], SIDE), wrap(second + slot[1], SIDE), part)
        return pltpu.make_async_remote_copy(
            src_ref=ref, dst_ref=ref,
            send_sem=self.send.at[self.number], recv_sem=self.recv.at[self.number, self.CLASS.get(number, 11)],
            device_id=self.target(half, *steps), device_id_type=MESH,
        )

    def bulk(self, kind, slots):
        ref = self.slots(slots)
        return pltpu.make_async_remote_copy(
            src_ref=ref, dst_ref=ref, send_sem=self.send.at[self.number], recv_sem=self.recv.at[self.number, kind],
            device_id=self.target(0, 1, 0), device_id_type=MESH,
        )

    def start(self, *numbers):
        for number in numbers:
            for half in range(2):
                self.copy(half, number).start()

    def arrived(self, number):
        self.bulk(self.CLASS[number], 1).wait_recv()

    def begin(self):
        self.start(0, 1, 4, 5)

    def second(self):
        self.arrived(0)
        self.start(2, 8, 9)
        self.arrived(1)
        self.start(3, 12, 13)
        self.arrived(4)
        self.start(6)
        self.arrived(5)
        self.start(7)

    def third(self):
        self.arrived(2)
        self.start(16, 17)
        for number in (8, 9, 12, 13):
            self.arrived(number)
            self.start(number + 2)

    def fourth(self):
        self.arrived(16)
        self.start(18)
        self.arrived(17)
        self.start(19)

    def finish(self):
        self.bulk(11, 4).wait_recv()

    def sent(self):
        self.bulk(0, PLANE - 1).wait_send()


def kernel(depth, teach_ref, draft_ref, teach_head_ref, draft_head_ref, kl_ref, grad_ref, rows, heads, extra,
           extra_low, mate_rows,
           teach_exp, draft_exp, table, plane_stats, depth_stats, plane_cross, depth_cross, total_stats, gap_own, gap_out, gap_mate, gap_in,
           kl_own, kl_in, total, far_sem, load_sem, low_send, low_recv, spread_send, spread_recv, head_send, head_recv, mate_send, mate_recv,
           piece_send, piece_recv, stat_send, stat_recv, gap_send, gap_recv, kl_send, kl_recv):
    teach_width = teach_ref.shape[1]
    draft_width = draft_ref.shape[1]
    width = teach_width + draft_width
    part = draft_width // 2
    vocab = teach_head_ref.shape[1]
    half_vocab = vocab // 2
    count = PLANE * RUN
    core = lax.axis_index("dp")
    z = lax.axis_index("tensor")
    context = lax.axis_index("context")
    y, x = context // SIDE, lax.rem(context, SIDE)
    other = 1 - core
    sequence = lax.rem(z, 2)
    above, below = wrap(z + 1, depth), wrap(z - 1, depth)
    mate = (other, z, context)
    here = pl.ds(pl.multiple_of(context * RUN, RUN), RUN)

    loads = [
        pltpu.make_async_copy(teach_head_ref, heads.at[0, pl.ds(0, teach_width)], load_sem.at[0]),
        pltpu.make_async_copy(draft_head_ref, heads.at[0, pl.ds(teach_width, draft_width)], load_sem.at[0]),
    ]

    def piece(index, group, owner):
        from_rows = pl.ds(pl.multiple_of(owner * 2 * RUN + group * RUN, RUN), RUN)
        source, columns = (
            (teach_ref, pl.ds(0, teach_width)), (draft_ref, pl.ds(teach_width, draft_width))
        )[index]
        return source.at[from_rows], rows.at[group, here, columns], group

    def extra_piece(index, owner):
        source = draft_ref.at[pl.ds(index * 2 * RUN + RUN, RUN), pl.ds(pl.multiple_of(owner * part, part), part)]
        return source, extra.at[context, pl.ds(index * RUN, RUN)], 2

    def local_copy(source, target, number):
        return pltpu.make_async_copy(source, target, load_sem.at[1 + number])

    def mate_copy(source, target, number):
        return pltpu.make_async_remote_copy(
            src_ref=source, dst_ref=target, send_sem=piece_send.at[0], recv_sem=piece_recv.at[number],
            device_id=mate, device_id_type=MESH,
        )

    pieces = [(index, group) for group in range(2) for index in range(2)]
    holds_rows = core == sequence
    group_rows = [rows.at[group, here, :] for group in range(2)]

    @pl.when(holds_rows)
    def _():
        for index, group in pieces:
            local_copy(*piece(index, group, core)).start()

    @pl.when(jnp.logical_not(holds_rows))
    def _():
        for index in range(2):
            local_copy(*extra_piece(index, core)).start()

    for load in loads:
        load.start()

    barrier = pltpu.get_barrier_semaphore()
    partners = [mate] + [(c, level, context) for c in (core, other) for level in (above, below)]
    partners += [(core, z, y * SIDE + wrap(x + step, SIDE)) for step in (1, -1)]
    partners += [(core, z, wrap(y + step, SIDE) * SIDE + x) for step in (1, -1)]
    for partner in partners:
        pl.semaphore_signal(barrier, inc=1, device_id=partner, device_id_type=MESH)
    pl.semaphore_wait(barrier, len(partners))

    @pl.when(holds_rows)
    def _():
        for index, group in pieces:
            mate_copy(*piece(index, group, other)).start()

    @pl.when(jnp.logical_not(holds_rows))
    def _():
        for index in range(2):
            mate_copy(*extra_piece(index, other)).start()

    where = (core, z, y, x)

    def group_place(group):
        return lambda slot, start, columns: rows.at[
            group, pl.ds(pl.multiple_of(slot * RUN, RUN), RUN), pl.ds(start, columns)]

    def group_slots(group):
        return lambda slots: rows.at[group, pl.ds(0, slots * RUN), :]

    first = Spread(group_place(0), group_slots(0), width, spread_send, spread_recv, 0, where)
    second = Spread(group_place(1), group_slots(1), width, spread_send, spread_recv, 1, where)
    third = Spread(lambda slot, start, columns: extra.at[slot, :, pl.ds(start, columns)],
                   lambda slots: extra.at[pl.ds(0, slots)], part, spread_send, spread_recv, 2, where)

    def rows_here(group):
        @pl.when(holds_rows)
        def _():
            local_copy(group_rows[group], group_rows[group], group).wait()

        @pl.when(jnp.logical_not(holds_rows))
        def _():
            mate_copy(group_rows[group], group_rows[group], group).wait_recv()

    def reach(number):
        step = 1 << number
        for level in (wrap(z + step, depth), wrap(z - step, depth)):
            pl.semaphore_signal(far_sem.at[number], inc=1, device_id=(core, level, context), device_id_type=MESH)

    def reached(number):
        pl.semaphore_wait(far_sem.at[number], 2)

    rows_here(0)
    first.begin()
    reach(0)
    pltpu.make_async_copy(heads.at[0], heads.at[0], load_sem.at[0]).wait()

    def head_copy(side, stage):
        depth_rows = width // 2
        half_rows = pl.ds(pl.multiple_of(core * depth_rows, depth_rows), depth_rows)
        columns = pl.ds(side * half_vocab, half_vocab)
        source = heads.at[0 if stage == 0 else 1, half_rows, columns]
        target = (core, (below, above)[side], context) if stage == 0 else mate
        return pltpu.make_async_remote_copy(
            src_ref=source, dst_ref=heads.at[1, half_rows, columns], send_sem=head_send.at[0],
            recv_sem=head_recv.at[stage], device_id=target, device_id_type=MESH,
        )

    def heads_all(ref, stage):
        return pltpu.make_async_remote_copy(src_ref=ref, dst_ref=ref, send_sem=head_send.at[0], recv_sem=head_recv.at[stage],
                                            device_id=mate, device_id_type=MESH)

    for side in range(2):
        head_copy(side, 0).start()

    first.second()
    first.third()
    rows_here(1)
    second.begin()
    reached(0)
    reach(1)
    first.fourth()
    first.finish()

    def low_copy(side, swap):
        half_count = count // 2
        some = pl.ds(side * half_count, half_count)
        goal = other if swap else core
        return pltpu.make_async_remote_copy(
            src_ref=rows.at[0, some, pl.ds(pl.multiple_of(teach_width + goal * part, part), part)],
            dst_ref=extra_low.at[core, some], send_sem=low_send.at[0], recv_sem=low_recv.at[0],
            device_id=(goal, (above, below)[side], context), device_id_type=MESH,
        )

    low_all = pltpu.make_async_remote_copy(
        src_ref=extra_low, dst_ref=extra_low, send_sem=low_send.at[0], recv_sem=low_recv.at[0],
        device_id=(core, above, context), device_id_type=MESH,
    )
    for side in range(2):
        for swap in range(2):
            low_copy(side, swap).start()

    def share_rows(group):
        return pltpu.make_async_remote_copy(
            src_ref=rows.at[group, :, pl.ds(pl.multiple_of(teach_width + other * part, part), part)],
            dst_ref=mate_rows.at[group], send_sem=mate_send.at[group], recv_sem=mate_recv.at[group],
            device_id=mate, device_id_type=MESH,
        )

    def logits(group, which):
        columns = pl.ds(which * vocab, vocab)
        teach_exp[group, :, columns] = jnp.dot(
            rows[group, :, :teach_width], heads[which, :teach_width, :], preferred_element_type=F32)
        draft_exp[group, :, columns] = jnp.dot(
            rows[group, :, teach_width:], heads[which, teach_width:, :], preferred_element_type=F32)

    block = 32

    def statistics(group):
        @pl.loop(0, count // block)
        def _(step):
            some = pl.ds(pl.multiple_of(step * block, block), block)
            teach = teach_exp[group, some, :]
            draft = draft_exp[group, some, :]
            teach_max = jnp.max(teach, axis=1, keepdims=True)
            draft_max = jnp.max(draft, axis=1, keepdims=True)
            teach_e = jnp.exp(teach - teach_max)
            draft_e = jnp.exp(draft - draft_max)
            teach_sum = jnp.sum(teach_e, axis=1, keepdims=True)
            cross_sum = jnp.sum(teach_e * (teach - draft), axis=1, keepdims=True)
            draft_sum = jnp.sum(draft_e, axis=1, keepdims=True)
            teach_exp[group, some, :] = teach_e
            draft_exp[group, some, :] = draft_e
            lane = lax.broadcasted_iota(jnp.int32, (block, 128), 1)
            wide = jnp.zeros((block, 128), F32)
            for position, value in ((0, teach_max), (1, draft_max), (2, teach_sum), (3, draft_sum), (10, cross_sum)):
                wide = jnp.where(lane == position, value, wide)
            table[some, :] = wide

        turned = jnp.transpose(table[...])
        for ref, row in ((plane_stats, 0), (plane_cross, 8)):
            ref[group, context, 0:4, :] = turned[row:row + 4, :count // 2]
            ref[group, context, 4:8, :] = turned[row:row + 4, count // 2:]

    level = z // 2
    levels = depth // 2
    hops = sorted(((dy, dx) for dy in range(SIDE) for dx in range(SIDE) if dy or dx),
                  key=lambda step: -min(step[0], SIDE - step[0]) - min(step[1], SIDE - step[1]))
    climbs = sorted(range(1, levels), key=lambda step: -min(step, levels - step))
    refs = (plane_stats, plane_cross, depth_stats, depth_cross)

    def stat_copy(group, kind, device, slots=None):
        own = context if kind < 2 else level
        ref = refs[kind].at[group, own if slots is None else pl.ds(0, slots)]
        return pltpu.make_async_remote_copy(
            src_ref=ref, dst_ref=ref, send_sem=stat_send.at[group, kind], recv_sem=stat_recv.at[group, kind],
            device_id=device, device_id_type=MESH,
        )

    def stat_all(group, kind):
        return stat_copy(group, kind, mate, PLANE - 1 if kind < 2 else levels - 1)

    def send_plane(group):
        for kind in range(2):
            for dy, dx in hops:
                stat_copy(group, kind, (core, z, wrap(y + dy, SIDE) * SIDE + wrap(x + dx, SIDE))).start()

    row = lax.broadcasted_iota(jnp.int32, (8, 128), 0)
    peaks = lax.rem(row, 4) < 2

    def merge(stats, crosses, group, members):
        tiles = [stats[group, member] for member in range(members)]
        peak = functools.reduce(jnp.maximum, tiles)
        scales = [pltpu.roll(jnp.exp(tile - peak), 2, 0) for tile in tiles]
        summed = functools.reduce(jnp.add, [tile * scale for tile, scale in zip(tiles, scales)])

        def cross():
            return functools.reduce(jnp.add, [crosses[group, member] * scales[member] for member in range(members)])

        return jnp.where(peaks, peak, summed), cross

    def send_depth(group):
        stat_all(group, 0).wait_recv()
        merged, cross = merge(plane_stats, plane_cross, group, PLANE)
        depth_stats[group, level] = merged
        for step in climbs:
            stat_copy(group, 2, (core, wrap(z + 2 * step, depth), context)).start()
        stat_all(group, 1).wait_recv()
        depth_cross[group, level] = cross()
        for step in climbs:
            stat_copy(group, 3, (core, wrap(z + 2 * step, depth), context)).start()

    def gap_copy(group, number):
        if number == 0:
            source, target, device = gap_own.at[group], gap_mate.at[group], mate
        else:
            side, swap = (number - 1) // 2, (number - 1) % 2
            source, target = gap_out.at[group, side], gap_in.at[core * 2 + group, side]
            device = (other if swap else core, (above, below)[side], context)
        return pltpu.make_async_remote_copy(
            src_ref=source, dst_ref=target, send_sem=gap_send.at[group], recv_sem=gap_recv.at[group, min(number, 1)],
            device_id=device, device_id_type=MESH,
        )

    def gap_all(group, blocks):
        ref = gap_in.at[pl.ds(0, blocks)]
        return pltpu.make_async_remote_copy(
            src_ref=ref, dst_ref=ref, send_sem=gap_send.at[group], recv_sem=gap_recv.at[group, 1],
            device_id=mate, device_id_type=MESH,
        )

    def gaps(group):
        stat_all(group, 2).wait_recv()
        merged, cross = merge(depth_stats, depth_cross, group, levels)
        factors = jnp.where(peaks, jnp.exp(plane_stats[group, context] - merged) / pltpu.roll(merged, 6, 0), 0.0)
        total_stats[...] = jnp.zeros_like(total_stats)
        total_stats[0:8, :count // 2] = factors
        total_stats[0:8, count // 2:] = pltpu.roll(factors, 4, 0)
        table[...] = jnp.transpose(total_stats[...])

        @pl.loop(0, count // block)
        def _(step):
            some = pl.ds(pl.multiple_of(step * block, block), block)
            factors = table[some, :]
            gap = (draft_exp[group, some, :] * factors[:, 1:2] - teach_exp[group, some, :] * factors[:, 0:1]).astype(BF16)
            gap_own[group, some, :] = gap[:, :vocab]
            gap_out[group, 0, some, :] = gap[:, vocab:vocab + half_vocab]
            gap_out[group, 1, some, :] = gap[:, vocab + half_vocab:]

        for number in (1, 2, 3, 4, 0):
            gap_copy(group, number).start()
        stat_all(group, 3).wait_recv()
        teach_max, draft_max = pltpu.roll(merged, 2, 0), pltpu.roll(merged, 1, 0)
        draft_total = pltpu.roll(merged, 7, 0)
        token_kl = cross() / merged - (teach_max + jnp.log(merged)) + (draft_max + jnp.log(draft_total))
        kl_own[group, :, :count // 2] = jnp.broadcast_to(token_kl[2:3], (8, count // 2))
        kl_own[group, :, count // 2:] = jnp.broadcast_to(token_kl[6:7], (8, count // 2))

    contract = (((0,), (0,)), ((), ()))

    def add(left, right, columns=slice(None), fresh=False):
        product = lax.dot_general(left, right, contract, preferred_element_type=F32)
        if fresh:
            total[:, columns] = product
        else:
            total[:, columns] += product

    def own_grad(group):
        mine = rows[group, :, pl.ds(pl.multiple_of(teach_width + core * part, part), part)]
        add(mine, gap_own[group], fresh=group == 0)

    def mate_grad(group):
        gap_copy(group, 0).wait_recv()
        add(mate_rows[group], gap_mate[group])

    def extra_grad(group):
        gap_all(group, 2).wait_recv()
        for owner in range(2):
            if group == 0:
                left = extra_low[owner]
            else:
                left = extra[:, owner * RUN:(owner + 1) * RUN, :].reshape(count, part)
            for side in range(2):
                add(left, gap_in[owner * 2 + group, side], slice(side * half_vocab, (side + 1) * half_vocab))

    reached(1)
    reach(2)
    second.second()
    share_rows(0).start()
    heads_all(heads.at[1, pl.ds(0, width // 2)], 0).wait_recv()
    for side in range(2):
        head_copy(side, 1).start()
    logits(0, 0)
    heads_all(heads.at[1, pl.ds(0, width // 2)], 1).wait_recv()
    logits(0, 1)
    statistics(0)
    send_plane(0)
    second.third()
    reached(2)
    send_depth(0)
    second.fourth()

    @pl.when(holds_rows)
    def _():
        mate_copy(extra.at[context], extra.at[context], 2).wait_recv()

    @pl.when(jnp.logical_not(holds_rows))
    def _():
        local_copy(extra.at[context], extra.at[context], 2).wait()

    third.begin()
    second.finish()
    share_rows(1).start()
    logits(1, 0)
    logits(1, 1)
    statistics(1)
    send_plane(1)
    third.second()
    gaps(0)
    send_depth(1)
    third.third()
    own_grad(0)
    share_rows(0).wait_recv()
    mate_grad(0)
    third.fourth()
    third.finish()
    low_all.wait_recv()
    extra_grad(0)
    gaps(1)

    def kl_copy(number, source_core):
        device = (sequence, (z, below)[number], context)
        return pltpu.make_async_remote_copy(
            src_ref=kl_own, dst_ref=kl_in.at[source_core], send_sem=kl_send.at[number],
            recv_sem=kl_recv.at[number], device_id=device, device_id_type=MESH,
        )

    kl_copy(1, core).start()

    @pl.when(jnp.logical_not(holds_rows))
    def _():
        kl_copy(0, core).start()

    own_grad(1)
    share_rows(1).wait_recv()
    mate_grad(1)

    @pl.when(holds_rows)
    def _():
        kl_copy(0, other).wait_recv()
        kl_in[core] = kl_own[...]

    @pl.when(jnp.logical_not(holds_rows))
    def _():
        pltpu.make_async_remote_copy(
            src_ref=kl_in, dst_ref=kl_in, send_sem=kl_send.at[1], recv_sem=kl_recv.at[1],
            device_id=mate, device_id_type=MESH,
        ).wait_recv()

    lane = lax.broadcasted_iota(jnp.int32, (8, count), 1)
    token_kl = jnp.zeros((8, count), F32)
    for owner in range(2):
        for group in range(2):
            start = (owner * 2 + group) * RUN
            moved = pltpu.roll(kl_in[owner, group], lax.rem(start - context * RUN + count, count), 1)
            token_kl = jnp.where((lane >= start) & (lane < start + RUN), moved, token_kl)
    kl_ref[...] = token_kl[0:1, 0:4 * RUN]

    extra_grad(1)
    grad_ref[...] = total[...].astype(grad_ref.dtype)

    first.sent()
    second.sent()
    third.sent()
    low_all.wait_send()
    heads_all(heads.at[1], 0).wait_send()

    @pl.when(holds_rows)
    def _():
        two = rows.at[0, pl.ds(0, 2 * RUN), :]
        mate_copy(two, two, 0).wait_send()

    @pl.when(jnp.logical_not(holds_rows))
    def _():
        mate_copy(extra.at[context], extra.at[context], 2).wait_send()
        kl_copy(0, core).wait_send()

    kl_copy(1, core).wait_send()
    for group in range(2):
        share_rows(group).wait_send()
        for kind in range(4):
            stat_all(group, kind).wait_send()
        gap_all(group, 3).wait_send()


def settle(kl_ref, grad_ref, kl_out, grad_out):
    kl_out[...] = kl_ref[...]
    grad_out[...] = grad_ref[...]


def local(depth, teacher_hidden, draft_hidden, teacher_head, draft_head):
    teach_width, vocab = teacher_head.shape
    draft_width = draft_head.shape[0]
    width, part = teach_width + draft_width, draft_width // 2
    count, levels = PLANE * RUN, depth // 2
    own_rows = teacher_hidden.shape[0]
    dma = pltpu.SemaphoreType.DMA
    scratch = [
        pltpu.VMEM((2, count, width), BF16),
        pltpu.VMEM((2, width, vocab), BF16),
        pltpu.VMEM((PLANE, own_rows // 2, part), BF16),
        pltpu.VMEM((2, count, part), BF16),
        pltpu.VMEM((2, count, part), BF16),
        pltpu.VMEM((2, count, 2 * vocab), F32),
        pltpu.VMEM((2, count, 2 * vocab), F32),
        pltpu.VMEM((count, 128), F32),
        pltpu.VMEM((2, PLANE, 8, 128), F32),
        pltpu.VMEM((2, levels, 8, 128), F32),
        pltpu.VMEM((2, PLANE, 8, 128), F32),
        pltpu.VMEM((2, levels, 8, 128), F32),
        pltpu.VMEM((128, count), F32),
        pltpu.VMEM((2, count, vocab), BF16),
        pltpu.VMEM((2, 2, count, vocab // 2), BF16),
        pltpu.VMEM((2, count, vocab), BF16),
        pltpu.VMEM((4, 2, count, vocab // 2), BF16),
        pltpu.VMEM((2, 8, count), F32),
        pltpu.VMEM((2, 2, 8, count), F32),
        pltpu.VMEM((part, vocab), F32),
        pltpu.SemaphoreType.REGULAR((3,)),
        dma((4,)),
        dma((1,)), dma((1,)),
        dma((3,)), dma((3, 12)),
        dma((1,)), dma((2,)),
        dma((2,)), dma((2,)),
        dma((1,)), dma((3,)),
        dma((2, 4)), dma((2, 4)),
        dma((2,)), dma((2, 2)),
        dma((2,)), dma((2,)),
    ]
    token_kl, head_grad = pl.pallas_call(
        functools.partial(kernel, depth),
        out_shape=(jax.ShapeDtypeStruct((1, own_rows), F32), jax.ShapeDtypeStruct((part, vocab), BF16)),
        in_specs=[pl.BlockSpec(memory_space=pl.ANY)] * 4,
        out_specs=(pl.BlockSpec(memory_space=pltpu.VMEM), pl.BlockSpec(memory_space=pltpu.VMEM)),
        scratch_shapes=scratch,
        compiler_params=pltpu.CompilerParams(collective_id=0, has_side_effects=True, vmem_limit_bytes=60 << 20),
        name="distill",
    )(teacher_hidden, draft_hidden, teacher_head, draft_head)
    token_kl, head_grad = pl.pallas_call(
        settle,
        out_shape=(jax.ShapeDtypeStruct((1, own_rows), F32), jax.ShapeDtypeStruct((part, vocab), BF16)),
        in_specs=[pl.BlockSpec(memory_space=pltpu.VMEM)] * 2,
        out_specs=(pl.BlockSpec(memory_space=pltpu.VMEM), pl.BlockSpec(memory_space=pltpu.VMEM)),
        name="settle",
    )(token_kl, head_grad)
    return token_kl.reshape(own_rows), head_grad


def solution(mesh):
    in_specs = (
        P(("dp", "context"), None),
        P(("dp", "context"), None),
        P(None, ("tensor", "context")),
        P(None, ("tensor", "context")),
    )
    out_specs = (P(("dp", "context")), P("dp", ("tensor", "context")))
    return jax.shard_map(
        functools.partial(local, mesh.shape["tensor"]), mesh=mesh, in_specs=in_specs, out_specs=out_specs, check_vma=False
    )
```

```python
import functools

import jax
import jax.numpy as jnp
from jax import lax
from jax.experimental import pallas as pl
from jax.experimental.pallas import tpu as pltpu
from jax.sharding import PartitionSpec as P

MESH = pl.DeviceIdType.MESH
F32 = jnp.float32
BF16 = jnp.bfloat16
SIDE = 4
PLANE = SIDE * SIDE
RUN = 16


def wrap(value, size):
    return lax.rem(value + size, size)


class Spread:
    CLASS = {0: 0, 1: 1, 4: 2, 5: 3, 8: 4, 9: 5, 12: 6, 13: 7, 2: 8, 3: 8, 16: 9, 17: 10}

    def __init__(self, place, slots, width, send, recv, number, where):
        self.slots = slots
        core, z, y, x = where
        self.core, self.z, self.send, self.recv, self.number = core, z, send, recv, number
        self.place, self.width = place, width
        self.axes = ((x, y), (y, x))

    def ref(self, half, first, second, part):
        slot = second * SIDE + first if half == 0 else first * SIDE + second
        columns = self.width // 2
        start = half * columns
        if part is None:
            return self.place(slot, start, columns)
        return self.place(slot, start + part * (columns // 2), columns // 2)

    def target(self, half, step_first, step_second):
        first, second = self.axes[half]
        first, second = wrap(first + step_first, SIDE), wrap(second + step_second, SIDE)
        context = second * SIDE + first if half == 0 else first * SIDE + second
        return (self.core, self.z, context)

    def plan(self, half, number):
        if number < 2:
            way = (1, -1)[number]
            return (0, 0), None, (way, 0)
        if number < 4:
            way = (1, -1)[number - 2]
            return (-way, 0), number - 2, (way, 0)
        offset = (0, -1, 1, 2)[(number - 4) // 4]
        kind = (number - 4) % 4
        way = (1, -1)[kind % 2]
        if kind < 2:
            return (offset, 0), None, (0, way)
        return (offset, -way), kind % 2, (0, way)

    def copy(self, half, number):
        slot, part, steps = self.plan(half, number)
        first, second = self.axes[half]
        ref = self.ref(half, wrap(first + slot[0], SIDE), wrap(second + slot[1], SIDE), part)
        return pltpu.make_async_remote_copy(
            src_ref=ref, dst_ref=ref,
            send_sem=self.send.at[self.number], recv_sem=self.recv.at[self.number, self.CLASS.get(number, 11)],
            device_id=self.target(half, *steps), device_id_type=MESH,
        )

    def bulk(self, kind, slots):
        ref = self.slots(slots)
        return pltpu.make_async_remote_copy(
            src_ref=ref, dst_ref=ref, send_sem=self.send.at[self.number], recv_sem=self.recv.at[self.number, kind],
            device_id=self.target(0, 1, 0), device_id_type=MESH,
        )

    def start(self, *numbers):
        for number in numbers:
            for half in range(2):
                self.copy(half, number).start()

    def arrived(self, number):
        self.bulk(self.CLASS[number], 1).wait_recv()

    def begin(self):
        self.start(0, 1, 4, 5)

    def second(self):
        self.arrived(0)
        self.start(2, 8, 9)
        self.arrived(1)
        self.start(3, 12, 13)
        self.arrived(4)
        self.start(6)
        self.arrived(5)
        self.start(7)

    def third(self):
        self.arrived(2)
        self.start(16, 17)
        for number in (8, 9, 12, 13):
            self.arrived(number)
            self.start(number + 2)

    def fourth(self):
        self.arrived(16)
        self.start(18)
        self.arrived(17)
        self.start(19)

    def finish(self):
        self.bulk(11, 4).wait_recv()

    def sent(self):
        self.bulk(0, PLANE - 1).wait_send()


def kernel(depth, teach_ref, draft_ref, teach_head_ref, draft_head_ref, kl_ref, grad_ref, rows, heads, extra,
           extra_low, mate_rows,
           teach_exp, draft_exp, table, plane_stats, depth_stats, plane_cross, depth_cross, total_stats, gap_own, gap_out, gap_mate, gap_in, turned,
           kl_own, kl_in, total, far_sem, load_sem, low_send, low_recv, spread_send, spread_recv, head_send, head_recv, mate_send, mate_recv,
           piece_send, piece_recv, stat_send, stat_recv, gap_send, gap_recv, kl_send, kl_recv):
    teach_width = teach_ref.shape[1]
    draft_width = draft_ref.shape[1]
    width = teach_width + draft_width
    part = draft_width // 2
    vocab = teach_head_ref.shape[1]
    half_vocab = vocab // 2
    count = PLANE * RUN
    core = lax.axis_index("dp")
    z = lax.axis_index("tensor")
    context = lax.axis_index("context")
    y, x = context // SIDE, lax.rem(context, SIDE)
    other = 1 - core
    sequence = lax.rem(z, 2)
    above, below = wrap(z + 1, depth), wrap(z - 1, depth)
    mate = (other, z, context)
    here = pl.ds(pl.multiple_of(context * RUN, RUN), RUN)

    loads = [
        pltpu.make_async_copy(teach_head_ref, heads.at[0, pl.ds(0, teach_width)], load_sem.at[0]),
        pltpu.make_async_copy(draft_head_ref, heads.at[0, pl.ds(teach_width, draft_width)], load_sem.at[0]),
    ]

    def piece(index, group, owner):
        from_rows = pl.ds(pl.multiple_of(owner * 2 * RUN + group * RUN, RUN), RUN)
        source, columns = (
            (teach_ref, pl.ds(0, teach_width)), (draft_ref, pl.ds(teach_width, draft_width))
        )[index]
        return source.at[from_rows], rows.at[group, here, columns], group

    def extra_piece(index, owner):
        source = draft_ref.at[pl.ds(index * 2 * RUN + RUN, RUN), pl.ds(pl.multiple_of(owner * part, part), part)]
        return source, extra.at[context, pl.ds(index * RUN, RUN)], 2

    def local_copy(source, target, number):
        return pltpu.make_async_copy(source, target, load_sem.at[1 + number])

    def mate_copy(source, target, number):
        return pltpu.make_async_remote_copy(
            src_ref=source, dst_ref=target, send_sem=piece_send.at[0], recv_sem=piece_recv.at[number],
            device_id=mate, device_id_type=MESH,
        )

    pieces = [(index, group) for group in range(2) for index in range(2)]
    holds_rows = core == sequence
    group_rows = [rows.at[group, here, :] for group in range(2)]

    @pl.when(holds_rows)
    def _():
        for index, group in pieces:
            local_copy(*piece(index, group, core)).start()

    @pl.when(jnp.logical_not(holds_rows))
    def _():
        for index in range(2):
            local_copy(*extra_piece(index, core)).start()

    for load in loads:
        load.start()

    barrier = pltpu.get_barrier_semaphore()
    partners = [mate] + [(c, level, context) for c in (core, other) for level in (above, below)]
    partners += [(core, z, y * SIDE + wrap(x + step, SIDE)) for step in (1, -1)]
    partners += [(core, z, wrap(y + step, SIDE) * SIDE + x) for step in (1, -1)]
    for partner in partners:
        pl.semaphore_signal(barrier, inc=1, device_id=partner, device_id_type=MESH)
    pl.semaphore_wait(barrier, len(partners))

    @pl.when(holds_rows)
    def _():
        for index, group in pieces:
            mate_copy(*piece(index, group, other)).start()

    @pl.when(jnp.logical_not(holds_rows))
    def _():
        for index in range(2):
            mate_copy(*extra_piece(index, other)).start()

    where = (core, z, y, x)

    def group_place(group):
        return lambda slot, start, columns: rows.at[
            group, pl.ds(pl.multiple_of(slot * RUN, RUN), RUN), pl.ds(start, columns)]

    def group_slots(group):
        return lambda slots: rows.at[group, pl.ds(0, slots * RUN), :]

    first = Spread(group_place(0), group_slots(0), width, spread_send, spread_recv, 0, where)
    second = Spread(group_place(1), group_slots(1), width, spread_send, spread_recv, 1, where)
    third = Spread(lambda slot, start, columns: extra.at[slot, :, pl.ds(start, columns)],
                   lambda slots: extra.at[pl.ds(0, slots)], part, spread_send, spread_recv, 2, where)

    def rows_here(group):
        @pl.when(holds_rows)
        def _():
            local_copy(group_rows[group], group_rows[group], group).wait()

        @pl.when(jnp.logical_not(holds_rows))
        def _():
            mate_copy(group_rows[group], group_rows[group], group).wait_recv()

    def reach(number):
        step = 1 << number
        for level in (wrap(z + step, depth), wrap(z - step, depth)):
            pl.semaphore_signal(far_sem.at[number], inc=1, device_id=(core, level, context), device_id_type=MESH)

    def reached(number):
        pl.semaphore_wait(far_sem.at[number], 2)

    rows_here(0)
    first.begin()
    reach(0)
    pltpu.make_async_copy(heads.at[0], heads.at[0], load_sem.at[0]).wait()

    def head_copy(side, stage):
        depth_rows = width // 2
        half_rows = pl.ds(pl.multiple_of(core * depth_rows, depth_rows), depth_rows)
        columns = pl.ds(side * half_vocab, half_vocab)
        source = heads.at[0 if stage == 0 else 1, half_rows, columns]
        target = (core, (below, above)[side], context) if stage == 0 else mate
        return pltpu.make_async_remote_copy(
            src_ref=source, dst_ref=heads.at[1, half_rows, columns], send_sem=head_send.at[0],
            recv_sem=head_recv.at[stage], device_id=target, device_id_type=MESH,
        )

    def heads_all(ref, stage):
        return pltpu.make_async_remote_copy(src_ref=ref, dst_ref=ref, send_sem=head_send.at[0], recv_sem=head_recv.at[stage],
                                            device_id=mate, device_id_type=MESH)

    for side in range(2):
        head_copy(side, 0).start()

    first.second()
    first.third()
    rows_here(1)
    second.begin()
    reached(0)
    reach(1)
    first.fourth()
    first.finish()

    def low_copy(side, swap):
        half_count = count // 2
        some = pl.ds(side * half_count, half_count)
        goal = other if swap else core
        return pltpu.make_async_remote_copy(
            src_ref=rows.at[0, some, pl.ds(pl.multiple_of(teach_width + goal * part, part), part)],
            dst_ref=extra_low.at[core, some], send_sem=low_send.at[0], recv_sem=low_recv.at[0],
            device_id=(goal, (above, below)[side], context), device_id_type=MESH,
        )

    low_all = pltpu.make_async_remote_copy(
        src_ref=extra_low, dst_ref=extra_low, send_sem=low_send.at[0], recv_sem=low_recv.at[0],
        device_id=(core, above, context), device_id_type=MESH,
    )
    for side in range(2):
        for swap in range(2):
            low_copy(side, swap).start()

    def share_rows(group):
        return pltpu.make_async_remote_copy(
            src_ref=rows.at[group, :, pl.ds(pl.multiple_of(teach_width + other * part, part), part)],
            dst_ref=mate_rows.at[group], send_sem=mate_send.at[group], recv_sem=mate_recv.at[group],
            device_id=mate, device_id_type=MESH,
        )

    def logits(group, which):
        columns = pl.ds(which * vocab, vocab)
        teach_exp[group, :, columns] = jnp.dot(
            rows[group, :, :teach_width], heads[which, :teach_width, :], preferred_element_type=F32)
        draft_exp[group, :, columns] = jnp.dot(
            rows[group, :, teach_width:], heads[which, teach_width:, :], preferred_element_type=F32)

    block = 32

    def statistics(group):
        @pl.loop(0, count // block)
        def _(step):
            some = pl.ds(pl.multiple_of(step * block, block), block)
            teach = teach_exp[group, some, :]
            draft = draft_exp[group, some, :]
            teach_max = jnp.max(teach, axis=1, keepdims=True)
            draft_max = jnp.max(draft, axis=1, keepdims=True)
            teach_e = jnp.exp(teach - teach_max)
            draft_e = jnp.exp(draft - draft_max)
            teach_sum = jnp.sum(teach_e, axis=1, keepdims=True)
            cross_sum = jnp.sum(teach_e * (teach - draft), axis=1, keepdims=True)
            draft_sum = jnp.sum(draft_e, axis=1, keepdims=True)
            teach_exp[group, some, :] = teach_e
            draft_exp[group, some, :] = draft_e
            lane = lax.broadcasted_iota(jnp.int32, (block, 128), 1)
            wide = jnp.zeros((block, 128), F32)
            for position, value in ((0, teach_max), (1, draft_max), (2, teach_sum), (3, draft_sum), (10, cross_sum)):
                wide = jnp.where(lane == position, value, wide)
            table[some, :] = wide

        turned = jnp.transpose(table[...])
        for ref, row in ((plane_stats, 0), (plane_cross, 8)):
            ref[group, context, 0:4, :] = turned[row:row + 4, :count // 2]
            ref[group, context, 4:8, :] = turned[row:row + 4, count // 2:]

    level = z // 2
    levels = depth // 2
    hops = sorted(((dy, dx) for dy in range(SIDE) for dx in range(SIDE) if dy or dx),
                  key=lambda step: -min(step[0], SIDE - step[0]) - min(step[1], SIDE - step[1]))
    climbs = sorted(range(1, levels), key=lambda step: -min(step, levels - step))
    refs = (plane_stats, plane_cross, depth_stats, depth_cross)

    def stat_copy(group, kind, device, slots=None):
        own = context if kind < 2 else level
        ref = refs[kind].at[group, own if slots is None else pl.ds(0, slots)]
        return pltpu.make_async_remote_copy(
            src_ref=ref, dst_ref=ref, send_sem=stat_send.at[group, kind], recv_sem=stat_recv.at[group, kind],
            device_id=device, device_id_type=MESH,
        )

    def stat_all(group, kind):
        return stat_copy(group, kind, mate, PLANE - 1 if kind < 2 else levels - 1)

    def send_plane(group):
        for kind in range(2):
            for dy, dx in hops:
                stat_copy(group, kind, (core, z, wrap(y + dy, SIDE) * SIDE + wrap(x + dx, SIDE))).start()

    row = lax.broadcasted_iota(jnp.int32, (8, 128), 0)
    peaks = lax.rem(row, 4) < 2

    def merge(stats, crosses, group, members):
        tiles = [stats[group, member] for member in range(members)]
        peak = functools.reduce(jnp.maximum, tiles)
        scales = [pltpu.roll(jnp.exp(tile - peak), 2, 0) for tile in tiles]
        summed = functools.reduce(jnp.add, [tile * scale for tile, scale in zip(tiles, scales)])

        def cross():
            return functools.reduce(jnp.add, [crosses[group, member] * scales[member] for member in range(members)])

        return jnp.where(peaks, peak, summed), cross

    def send_depth(group):
        stat_all(group, 0).wait_recv()
        merged, cross = merge(plane_stats, plane_cross, group, PLANE)
        depth_stats[group, level] = merged
        for step in climbs:
            stat_copy(group, 2, (core, wrap(z + 2 * step, depth), context)).start()
        stat_all(group, 1).wait_recv()
        depth_cross[group, level] = cross()
        for step in climbs:
            stat_copy(group, 3, (core, wrap(z + 2 * step, depth), context)).start()

    def gap_copy(group, number):
        if number == 0:
            source, target, device = gap_own.at[group], gap_mate.at[group], mate
        else:
            side, swap = (number - 1) // 2, (number - 1) % 2
            source = gap_out.at[group, side]
            target = gap_in.at[core * 2 + group, :, pl.ds(side * half_vocab, half_vocab)]
            device = (other if swap else core, (above, below)[side], context)
        return pltpu.make_async_remote_copy(
            src_ref=source, dst_ref=target, send_sem=gap_send.at[group], recv_sem=gap_recv.at[group, min(number, 1)],
            device_id=device, device_id_type=MESH,
        )

    def gap_all(group, blocks):
        ref = gap_in.at[pl.ds(0, blocks)]
        return pltpu.make_async_remote_copy(
            src_ref=ref, dst_ref=ref, send_sem=gap_send.at[group], recv_sem=gap_recv.at[group, 1],
            device_id=mate, device_id_type=MESH,
        )

    def gaps(group):
        stat_all(group, 2).wait_recv()
        merged, cross = merge(depth_stats, depth_cross, group, levels)
        factors = jnp.where(peaks, jnp.exp(plane_stats[group, context] - merged) / pltpu.roll(merged, 6, 0), 0.0)
        total_stats[...] = jnp.zeros_like(total_stats)
        total_stats[0:8, :count // 2] = factors
        total_stats[0:8, count // 2:] = pltpu.roll(factors, 4, 0)
        table[...] = jnp.transpose(total_stats[...])

        @pl.loop(0, count // block)
        def _(step):
            some = pl.ds(pl.multiple_of(step * block, block), block)
            factors = table[some, :]
            gap = (draft_exp[group, some, :] * factors[:, 1:2] - teach_exp[group, some, :] * factors[:, 0:1]).astype(BF16)
            gap_own[group, some, :] = gap[:, :vocab]
            gap_out[group, 0, some, :] = gap[:, vocab:vocab + half_vocab]
            gap_out[group, 1, some, :] = gap[:, vocab + half_vocab:]

        for number in (1, 2, 3, 4, 0):
            gap_copy(group, number).start()
        stat_all(group, 3).wait_recv()
        teach_max, draft_max = pltpu.roll(merged, 2, 0), pltpu.roll(merged, 1, 0)
        draft_total = pltpu.roll(merged, 7, 0)
        token_kl = cross() / merged - (teach_max + jnp.log(merged)) + (draft_max + jnp.log(draft_total))
        kl_own[group, :, :count // 2] = jnp.broadcast_to(token_kl[2:3], (8, count // 2))
        kl_own[group, :, count // 2:] = jnp.broadcast_to(token_kl[6:7], (8, count // 2))

    contract = (((0,), (0,)), ((), ()))

    def add(left, right, columns=slice(None), fresh=False):
        product = lax.dot_general(left, right, contract, preferred_element_type=F32)
        if fresh:
            total[:, columns] = product
        else:
            total[:, columns] += product

    def own_grad(group):
        mine = rows[group, :, pl.ds(pl.multiple_of(teach_width + core * part, part), part)]
        add(mine, gap_own[group], fresh=group == 0)

    def mate_grad(group):
        gap_copy(group, 0).wait_recv()
        add(mate_rows[group], gap_mate[group])

    def extra_grad(group):
        gap_all(group, 2).wait_recv()
        for owner in range(2):
            right = gap_in[owner * 2 + group]
            if group == 0:
                add(extra_low[owner], right)
            else:
                total[...] += jnp.dot(turned[owner], right, preferred_element_type=F32)

    reached(1)
    reach(2)
    second.second()
    share_rows(0).start()
    heads_all(heads.at[1, pl.ds(0, width // 2)], 0).wait_recv()
    for side in range(2):
        head_copy(side, 1).start()
    logits(0, 0)
    heads_all(heads.at[1, pl.ds(0, width // 2)], 1).wait_recv()
    logits(0, 1)
    statistics(0)
    send_plane(0)
    second.third()
    reached(2)
    send_depth(0)
    second.fourth()

    @pl.when(holds_rows)
    def _():
        mate_copy(extra.at[context], extra.at[context], 2).wait_recv()

    @pl.when(jnp.logical_not(holds_rows))
    def _():
        local_copy(extra.at[context], extra.at[context], 2).wait()

    third.begin()
    second.finish()
    share_rows(1).start()
    logits(1, 0)
    logits(1, 1)
    statistics(1)
    send_plane(1)
    third.second()
    gaps(0)
    send_depth(1)
    third.third()
    own_grad(0)
    share_rows(0).wait_recv()
    mate_grad(0)
    third.fourth()
    third.finish()
    low_all.wait_recv()
    extra_grad(0)
    for owner in range(2):
        turned[owner] = jnp.transpose(extra[:, owner * RUN:(owner + 1) * RUN, :].reshape(count, part))
    gaps(1)

    def kl_copy(number, source_core):
        device = (sequence, (z, below)[number], context)
        return pltpu.make_async_remote_copy(
            src_ref=kl_own, dst_ref=kl_in.at[source_core], send_sem=kl_send.at[number],
            recv_sem=kl_recv.at[number], device_id=device, device_id_type=MESH,
        )

    kl_copy(1, core).start()

    @pl.when(jnp.logical_not(holds_rows))
    def _():
        kl_copy(0, core).start()

    own_grad(1)
    share_rows(1).wait_recv()
    mate_grad(1)

    @pl.when(holds_rows)
    def _():
        kl_copy(0, other).wait_recv()
        kl_in[core] = kl_own[...]

    @pl.when(jnp.logical_not(holds_rows))
    def _():
        pltpu.make_async_remote_copy(
            src_ref=kl_in, dst_ref=kl_in, send_sem=kl_send.at[1], recv_sem=kl_recv.at[1],
            device_id=mate, device_id_type=MESH,
        ).wait_recv()

    lane = lax.broadcasted_iota(jnp.int32, (8, count), 1)
    token_kl = jnp.zeros((8, count), F32)
    for owner in range(2):
        for group in range(2):
            start = (owner * 2 + group) * RUN
            moved = pltpu.roll(kl_in[owner, group], lax.rem(start - context * RUN + count, count), 1)
            token_kl = jnp.where((lane >= start) & (lane < start + RUN), moved, token_kl)
    kl_ref[...] = token_kl[0:1, 0:4 * RUN]

    extra_grad(1)
    grad_ref[...] = total[...].astype(grad_ref.dtype)

    first.sent()
    second.sent()
    third.sent()
    low_all.wait_send()
    heads_all(heads.at[1], 0).wait_send()

    @pl.when(holds_rows)
    def _():
        two = rows.at[0, pl.ds(0, 2 * RUN), :]
        mate_copy(two, two, 0).wait_send()

    @pl.when(jnp.logical_not(holds_rows))
    def _():
        mate_copy(extra.at[context], extra.at[context], 2).wait_send()
        kl_copy(0, core).wait_send()

    kl_copy(1, core).wait_send()
    for group in range(2):
        share_rows(group).wait_send()
        for kind in range(4):
            stat_all(group, kind).wait_send()
        gap_all(group, 3).wait_send()


def settle(kl_ref, grad_ref, kl_out, grad_out, sem):
    copies = [
        pltpu.make_async_copy(grad_ref, grad_out, sem.at[0]),
        pltpu.make_async_copy(kl_ref, kl_out, sem.at[1]),
    ]
    for copy in copies:
        copy.start()
    for copy in copies:
        copy.wait()


def local(depth, teacher_hidden, draft_hidden, teacher_head, draft_head):
    teach_width, vocab = teacher_head.shape
    draft_width = draft_head.shape[0]
    width, part = teach_width + draft_width, draft_width // 2
    count, levels = PLANE * RUN, depth // 2
    own_rows = teacher_hidden.shape[0]
    dma = pltpu.SemaphoreType.DMA
    scratch = [
        pltpu.VMEM((2, count, width), BF16),
        pltpu.VMEM((2, width, vocab), BF16),
        pltpu.VMEM((PLANE, own_rows // 2, part), BF16),
        pltpu.VMEM((2, count, part), BF16),
        pltpu.VMEM((2, count, part), BF16),
        pltpu.VMEM((2, count, 2 * vocab), F32),
        pltpu.VMEM((2, count, 2 * vocab), F32),
        pltpu.VMEM((count, 128), F32),
        pltpu.VMEM((2, PLANE, 8, 128), F32),
        pltpu.VMEM((2, levels, 8, 128), F32),
        pltpu.VMEM((2, PLANE, 8, 128), F32),
        pltpu.VMEM((2, levels, 8, 128), F32),
        pltpu.VMEM((128, count), F32),
        pltpu.VMEM((2, count, vocab), BF16),
        pltpu.VMEM((2, 2, count, vocab // 2), BF16),
        pltpu.VMEM((2, count, vocab), BF16),
        pltpu.VMEM((4, count, vocab), BF16),
        pltpu.VMEM((2, part, count), BF16),
        pltpu.VMEM((2, 8, count), F32),
        pltpu.VMEM((2, 2, 8, count), F32),
        pltpu.VMEM((part, vocab), F32),
        pltpu.SemaphoreType.REGULAR((3,)),
        dma((4,)),
        dma((1,)), dma((1,)),
        dma((3,)), dma((3, 12)),
        dma((1,)), dma((2,)),
        dma((2,)), dma((2,)),
        dma((1,)), dma((3,)),
        dma((2, 4)), dma((2, 4)),
        dma((2,)), dma((2, 2)),
        dma((2,)), dma((2,)),
    ]
    token_kl, head_grad = pl.pallas_call(
        functools.partial(kernel, depth),
        out_shape=(pltpu.VMEM((1, own_rows), F32), pltpu.VMEM((part, vocab), BF16)),
        in_specs=[pl.BlockSpec(memory_space=pl.ANY)] * 4,
        out_specs=(pl.BlockSpec(memory_space=pltpu.VMEM), pl.BlockSpec(memory_space=pltpu.VMEM)),
        scratch_shapes=scratch,
        compiler_params=pltpu.CompilerParams(collective_id=0, has_side_effects=True, vmem_limit_bytes=60 << 20),
        name="distill",
    )(teacher_hidden, draft_hidden, teacher_head, draft_head)
    token_kl, head_grad = pl.pallas_call(
        settle,
        out_shape=(pltpu.HBM((1, own_rows), F32), pltpu.HBM((part, vocab), BF16)),
        in_specs=[pl.BlockSpec(memory_space=pltpu.VMEM)] * 2,
        out_specs=(pl.BlockSpec(memory_space=pltpu.HBM), pl.BlockSpec(memory_space=pltpu.HBM)),
        scratch_shapes=[pltpu.SemaphoreType.DMA((2,))],
        compiler_params=pltpu.CompilerParams(vmem_limit_bytes=8 << 20),
        name="settle",
    )(token_kl, head_grad)
    return token_kl.reshape(own_rows), head_grad


def solution(mesh):
    in_specs = (
        P(("dp", "context"), None),
        P(("dp", "context"), None),
        P(None, ("tensor", "context")),
        P(None, ("tensor", "context")),
    )
    out_specs = (P(("dp", "context")), P("dp", ("tensor", "context")))
    return jax.shard_map(
        functools.partial(local, mesh.shape["tensor"]), mesh=mesh, in_specs=in_specs, out_specs=out_specs, check_vma=False
    )
```

```python
import functools

import jax
import jax.numpy as jnp
from jax import lax
from jax.experimental import pallas as pl
from jax.experimental.pallas import tpu as pltpu
from jax.sharding import PartitionSpec as P

MESH = pl.DeviceIdType.MESH
F32 = jnp.float32
BF16 = jnp.bfloat16
SIDE = 4
PLANE = SIDE * SIDE
RUN = 16


def wrap(value, size):
    return lax.rem(value + size, size)


class Spread:
    CLASS = {0: 0, 1: 1, 4: 2, 5: 3, 8: 4, 9: 5, 12: 6, 13: 7, 2: 8, 3: 8, 16: 9, 17: 10}

    def __init__(self, place, slots, width, send, recv, number, where):
        self.slots = slots
        core, z, y, x = where
        self.core, self.z, self.send, self.recv, self.number = core, z, send, recv, number
        self.place, self.width = place, width
        self.axes = ((x, y), (y, x))

    def ref(self, half, first, second, part):
        slot = second * SIDE + first if half == 0 else first * SIDE + second
        columns = self.width // 2
        start = half * columns
        if part is None:
            return self.place(slot, start, columns)
        return self.place(slot, start + part * (columns // 2), columns // 2)

    def target(self, half, step_first, step_second):
        first, second = self.axes[half]
        first, second = wrap(first + step_first, SIDE), wrap(second + step_second, SIDE)
        context = second * SIDE + first if half == 0 else first * SIDE + second
        return (self.core, self.z, context)

    def plan(self, half, number):
        if number < 2:
            way = (1, -1)[number]
            return (0, 0), None, (way, 0)
        if number < 4:
            way = (1, -1)[number - 2]
            return (-way, 0), number - 2, (way, 0)
        offset = (0, -1, 1, 2)[(number - 4) // 4]
        kind = (number - 4) % 4
        way = (1, -1)[kind % 2]
        if kind < 2:
            return (offset, 0), None, (0, way)
        return (offset, -way), kind % 2, (0, way)

    def copy(self, half, number):
        slot, part, steps = self.plan(half, number)
        first, second = self.axes[half]
        ref = self.ref(half, wrap(first + slot[0], SIDE), wrap(second + slot[1], SIDE), part)
        return pltpu.make_async_remote_copy(
            src_ref=ref, dst_ref=ref,
            send_sem=self.send.at[self.number], recv_sem=self.recv.at[self.number, self.CLASS.get(number, 11)],
            device_id=self.target(half, *steps), device_id_type=MESH,
        )

    def bulk(self, kind, slots):
        ref = self.slots(slots)
        return pltpu.make_async_remote_copy(
            src_ref=ref, dst_ref=ref, send_sem=self.send.at[self.number], recv_sem=self.recv.at[self.number, kind],
            device_id=self.target(0, 1, 0), device_id_type=MESH,
        )

    def start(self, *numbers):
        for number in numbers:
            for half in range(2):
                self.copy(half, number).start()

    def arrived(self, number):
        self.bulk(self.CLASS[number], 1).wait_recv()

    def begin(self):
        self.start(0, 1, 4, 5)

    def second(self):
        self.arrived(0)
        self.start(2, 8, 9)
        self.arrived(1)
        self.start(3, 12, 13)
        self.arrived(4)
        self.start(6)
        self.arrived(5)
        self.start(7)

    def third(self):
        self.arrived(2)
        self.start(16, 17)
        for number in (8, 9, 12, 13):
            self.arrived(number)
            self.start(number + 2)

    def fourth(self):
        self.arrived(16)
        self.start(18)
        self.arrived(17)
        self.start(19)

    def finish(self):
        self.bulk(11, 4).wait_recv()

    def sent(self):
        self.bulk(0, PLANE - 1).wait_send()


def kernel(depth, teach_ref, draft_ref, teach_head_ref, draft_head_ref, kl_ref, grad_ref, rows, heads, extra,
           extra_low, mate_rows,
           teach_exp, draft_exp, table, plane_stats, depth_stats, plane_cross, depth_cross, total_stats, gap_own, gap_out, gap_mate, gap_in, turned,
           kl_own, kl_in, total, far_sem, load_sem, low_send, low_recv, spread_send, spread_recv, head_send, head_recv, mate_send, mate_recv,
           piece_send, piece_recv, stat_send, stat_recv, gap_send, gap_recv, kl_send, kl_recv):
    teach_width = teach_ref.shape[1]
    draft_width = draft_ref.shape[1]
    width = teach_width + draft_width
    part = draft_width // 2
    vocab = teach_head_ref.shape[1]
    half_vocab = vocab // 2
    count = PLANE * RUN
    core = lax.axis_index("dp")
    z = lax.axis_index("tensor")
    context = lax.axis_index("context")
    y, x = context // SIDE, lax.rem(context, SIDE)
    other = 1 - core
    sequence = lax.rem(z, 2)
    above, below = wrap(z + 1, depth), wrap(z - 1, depth)
    mate = (other, z, context)
    here = pl.ds(pl.multiple_of(context * RUN, RUN), RUN)

    loads = [
        pltpu.make_async_copy(teach_head_ref, heads.at[0, pl.ds(0, teach_width)], load_sem.at[0]),
        pltpu.make_async_copy(draft_head_ref, heads.at[0, pl.ds(teach_width, draft_width)], load_sem.at[0]),
    ]

    def piece(index, group, owner):
        from_rows = pl.ds(pl.multiple_of(owner * 2 * RUN + group * RUN, RUN), RUN)
        source, columns = (
            (teach_ref, pl.ds(0, teach_width)), (draft_ref, pl.ds(teach_width, draft_width))
        )[index]
        return source.at[from_rows], rows.at[group, here, columns], group

    def extra_piece(index, owner):
        source = draft_ref.at[pl.ds(index * 2 * RUN + RUN, RUN), pl.ds(pl.multiple_of(owner * part, part), part)]
        return source, extra.at[context, pl.ds(index * RUN, RUN)], 2

    def local_copy(source, target, number):
        return pltpu.make_async_copy(source, target, load_sem.at[1 + number])

    def mate_copy(source, target, number):
        return pltpu.make_async_remote_copy(
            src_ref=source, dst_ref=target, send_sem=piece_send.at[0], recv_sem=piece_recv.at[number],
            device_id=mate, device_id_type=MESH,
        )

    pieces = [(index, group) for group in range(2) for index in range(2)]
    holds_rows = core == sequence
    group_rows = [rows.at[group, here, :] for group in range(2)]

    @pl.when(holds_rows)
    def _():
        for index, group in pieces:
            local_copy(*piece(index, group, core)).start()

    @pl.when(jnp.logical_not(holds_rows))
    def _():
        for index in range(2):
            local_copy(*extra_piece(index, core)).start()

    for load in loads:
        load.start()

    barrier = pltpu.get_barrier_semaphore()
    partners = [mate] + [(c, level, context) for c in (core, other) for level in (above, below)]
    partners += [(core, z, y * SIDE + wrap(x + step, SIDE)) for step in (1, -1)]
    partners += [(core, z, wrap(y + step, SIDE) * SIDE + x) for step in (1, -1)]
    for partner in partners:
        pl.semaphore_signal(barrier, inc=1, device_id=partner, device_id_type=MESH)
    pl.semaphore_wait(barrier, len(partners))

    @pl.when(holds_rows)
    def _():
        for index, group in pieces:
            mate_copy(*piece(index, group, other)).start()

    @pl.when(jnp.logical_not(holds_rows))
    def _():
        for index in range(2):
            mate_copy(*extra_piece(index, other)).start()

    where = (core, z, y, x)

    def group_place(group):
        return lambda slot, start, columns: rows.at[
            group, pl.ds(pl.multiple_of(slot * RUN, RUN), RUN), pl.ds(start, columns)]

    def group_slots(group):
        return lambda slots: rows.at[group, pl.ds(0, slots * RUN), :]

    first = Spread(group_place(0), group_slots(0), width, spread_send, spread_recv, 0, where)
    second = Spread(group_place(1), group_slots(1), width, spread_send, spread_recv, 1, where)
    third = Spread(lambda slot, start, columns: extra.at[slot, :, pl.ds(start, columns)],
                   lambda slots: extra.at[pl.ds(0, slots)], part, spread_send, spread_recv, 2, where)

    def rows_here(group):
        @pl.when(holds_rows)
        def _():
            local_copy(group_rows[group], group_rows[group], group).wait()

        @pl.when(jnp.logical_not(holds_rows))
        def _():
            mate_copy(group_rows[group], group_rows[group], group).wait_recv()

    def reach(number):
        step = 1 << number
        for level in (wrap(z + step, depth), wrap(z - step, depth)):
            pl.semaphore_signal(far_sem.at[number], inc=1, device_id=(core, level, context), device_id_type=MESH)

    def reached(number):
        pl.semaphore_wait(far_sem.at[number], 2)

    rows_here(0)
    first.begin()
    reach(0)
    pltpu.make_async_copy(heads.at[0], heads.at[0], load_sem.at[0]).wait()

    def head_copy(side, stage):
        depth_rows = width // 2
        half_rows = pl.ds(pl.multiple_of(core * depth_rows, depth_rows), depth_rows)
        columns = pl.ds(side * half_vocab, half_vocab)
        source = heads.at[0 if stage == 0 else 1, half_rows, columns]
        target = (core, (below, above)[side], context) if stage == 0 else mate
        return pltpu.make_async_remote_copy(
            src_ref=source, dst_ref=heads.at[1, half_rows, columns], send_sem=head_send.at[0],
            recv_sem=head_recv.at[stage], device_id=target, device_id_type=MESH,
        )

    def heads_all(ref, stage):
        return pltpu.make_async_remote_copy(src_ref=ref, dst_ref=ref, send_sem=head_send.at[0], recv_sem=head_recv.at[stage],
                                            device_id=mate, device_id_type=MESH)

    for side in range(2):
        head_copy(side, 0).start()

    first.second()
    first.third()
    rows_here(1)
    second.begin()
    reached(0)
    reach(1)
    first.fourth()
    first.finish()

    def low_copy(side, swap):
        half_count = count // 2
        some = pl.ds(side * half_count, half_count)
        goal = other if swap else core
        return pltpu.make_async_remote_copy(
            src_ref=rows.at[0, some, pl.ds(pl.multiple_of(teach_width + goal * part, part), part)],
            dst_ref=extra_low.at[core, some], send_sem=low_send.at[0], recv_sem=low_recv.at[0],
            device_id=(goal, (above, below)[side], context), device_id_type=MESH,
        )

    low_all = pltpu.make_async_remote_copy(
        src_ref=extra_low, dst_ref=extra_low, send_sem=low_send.at[0], recv_sem=low_recv.at[0],
        device_id=(core, above, context), device_id_type=MESH,
    )
    for side in range(2):
        for swap in range(2):
            low_copy(side, swap).start()

    def share_rows(group):
        return pltpu.make_async_remote_copy(
            src_ref=rows.at[group, :, pl.ds(pl.multiple_of(teach_width + other * part, part), part)],
            dst_ref=mate_rows.at[group], send_sem=mate_send.at[group], recv_sem=mate_recv.at[group],
            device_id=mate, device_id_type=MESH,
        )

    def logits(group, which):
        columns = pl.ds(which * vocab, vocab)
        teach_exp[group, :, columns] = jnp.dot(
            rows[group, :, :teach_width], heads[which, :teach_width, :], preferred_element_type=F32)
        draft_exp[group, :, columns] = jnp.dot(
            rows[group, :, teach_width:], heads[which, teach_width:, :], preferred_element_type=F32)

    block = 32

    def statistics(group):
        @pl.loop(0, count // block)
        def _(step):
            some = pl.ds(pl.multiple_of(step * block, block), block)
            teach = teach_exp[group, some, :]
            draft = draft_exp[group, some, :]
            teach_max = jnp.max(teach, axis=1, keepdims=True)
            draft_max = jnp.max(draft, axis=1, keepdims=True)
            teach_e = jnp.exp(teach - teach_max)
            draft_e = jnp.exp(draft - draft_max)
            teach_sum = jnp.sum(teach_e, axis=1, keepdims=True)
            cross_sum = jnp.sum(teach_e * (teach - draft), axis=1, keepdims=True)
            draft_sum = jnp.sum(draft_e, axis=1, keepdims=True)
            teach_exp[group, some, :] = teach_e
            draft_exp[group, some, :] = draft_e
            lane = lax.broadcasted_iota(jnp.int32, (block, 128), 1)
            wide = jnp.zeros((block, 128), F32)
            for position, value in ((0, teach_max), (1, draft_max), (2, teach_sum), (3, draft_sum), (10, cross_sum)):
                wide = jnp.where(lane == position, value, wide)
            table[some, :] = wide

        turned = jnp.transpose(table[...])
        for ref, row in ((plane_stats, 0), (plane_cross, 8)):
            ref[group, context, 0:4, :] = turned[row:row + 4, :count // 2]
            ref[group, context, 4:8, :] = turned[row:row + 4, count // 2:]

    level = z // 2
    levels = depth // 2
    hops = sorted(((dy, dx) for dy in range(SIDE) for dx in range(SIDE) if dy or dx),
                  key=lambda step: -min(step[0], SIDE - step[0]) - min(step[1], SIDE - step[1]))
    climbs = sorted(range(1, levels), key=lambda step: -min(step, levels - step))
    refs = (plane_stats, plane_cross, depth_stats, depth_cross)

    def stat_copy(group, kind, device, slots=None):
        own = context if kind < 2 else level
        ref = refs[kind].at[group, own if slots is None else pl.ds(0, slots)]
        return pltpu.make_async_remote_copy(
            src_ref=ref, dst_ref=ref, send_sem=stat_send.at[group, kind], recv_sem=stat_recv.at[group, kind],
            device_id=device, device_id_type=MESH,
        )

    def stat_all(group, kind):
        return stat_copy(group, kind, mate, PLANE - 1 if kind < 2 else levels - 1)

    def send_plane(group):
        for kind in range(2):
            for dy, dx in hops:
                stat_copy(group, kind, (core, z, wrap(y + dy, SIDE) * SIDE + wrap(x + dx, SIDE))).start()

    row = lax.broadcasted_iota(jnp.int32, (8, 128), 0)
    peaks = lax.rem(row, 4) < 2

    def merge(stats, crosses, group, members):
        tiles = [stats[group, member] for member in range(members)]
        peak = functools.reduce(jnp.maximum, tiles)
        scales = [pltpu.roll(jnp.exp(tile - peak), 2, 0) for tile in tiles]
        summed = functools.reduce(jnp.add, [tile * scale for tile, scale in zip(tiles, scales)])

        def cross():
            return functools.reduce(jnp.add, [crosses[group, member] * scales[member] for member in range(members)])

        return jnp.where(peaks, peak, summed), cross

    def send_depth(group):
        stat_all(group, 0).wait_recv()
        merged, cross = merge(plane_stats, plane_cross, group, PLANE)
        depth_stats[group, level] = merged
        for step in climbs:
            stat_copy(group, 2, (core, wrap(z + 2 * step, depth), context)).start()
        stat_all(group, 1).wait_recv()
        depth_cross[group, level] = cross()
        for step in climbs:
            stat_copy(group, 3, (core, wrap(z + 2 * step, depth), context)).start()

    def gap_copy(group, number):
        if number == 0:
            source, target, device = gap_own.at[group], gap_mate.at[group], mate
        else:
            side, swap = (number - 1) // 2, (number - 1) % 2
            source = gap_out.at[group, side]
            target = gap_in.at[core * 2 + group, :, pl.ds(side * half_vocab, half_vocab)]
            device = (other if swap else core, (above, below)[side], context)
        return pltpu.make_async_remote_copy(
            src_ref=source, dst_ref=target, send_sem=gap_send.at[group], recv_sem=gap_recv.at[group, min(number, 1)],
            device_id=device, device_id_type=MESH,
        )

    def gap_all(group, blocks):
        ref = gap_in.at[pl.ds(0, blocks)]
        return pltpu.make_async_remote_copy(
            src_ref=ref, dst_ref=ref, send_sem=gap_send.at[group], recv_sem=gap_recv.at[group, 1],
            device_id=mate, device_id_type=MESH,
        )

    def gaps(group):
        stat_all(group, 2).wait_recv()
        merged, cross = merge(depth_stats, depth_cross, group, levels)
        factors = jnp.where(peaks, jnp.exp(plane_stats[group, context] - merged) / pltpu.roll(merged, 6, 0), 0.0)
        total_stats[...] = jnp.zeros_like(total_stats)
        total_stats[0:8, :count // 2] = factors
        total_stats[0:8, count // 2:] = pltpu.roll(factors, 4, 0)
        table[...] = jnp.transpose(total_stats[...])

        @pl.loop(0, count // block)
        def _(step):
            some = pl.ds(pl.multiple_of(step * block, block), block)
            factors = table[some, :]
            gap = (draft_exp[group, some, :] * factors[:, 1:2] - teach_exp[group, some, :] * factors[:, 0:1]).astype(BF16)
            gap_own[group, some, :] = gap[:, :vocab]
            gap_out[group, 0, some, :] = gap[:, vocab:vocab + half_vocab]
            gap_out[group, 1, some, :] = gap[:, vocab + half_vocab:]

        for number in (1, 2, 3, 4, 0):
            gap_copy(group, number).start()
        stat_all(group, 3).wait_recv()
        teach_max, draft_max = pltpu.roll(merged, 2, 0), pltpu.roll(merged, 1, 0)
        draft_total = pltpu.roll(merged, 7, 0)
        token_kl = cross() / merged - (teach_max + jnp.log(merged)) + (draft_max + jnp.log(draft_total))
        kl_own[group, :, :count // 2] = jnp.broadcast_to(token_kl[2:3], (8, count // 2))
        kl_own[group, :, count // 2:] = jnp.broadcast_to(token_kl[6:7], (8, count // 2))

    contract = (((0,), (0,)), ((), ()))

    def add(left, right, columns=slice(None), fresh=False):
        product = lax.dot_general(left, right, contract, preferred_element_type=F32)
        if fresh:
            total[:, columns] = product
        else:
            total[:, columns] += product

    def own_grad(group):
        mine = rows[group, :, pl.ds(pl.multiple_of(teach_width + core * part, part), part)]
        add(mine, gap_own[group], fresh=group == 0)

    def mate_grad(group):
        gap_copy(group, 0).wait_recv()
        add(mate_rows[group], gap_mate[group])

    def extra_grad(group):
        gap_all(group, 2).wait_recv()
        for owner in range(2):
            right = gap_in[owner * 2 + group]
            if group == 0:
                add(extra_low[owner], right)
            else:
                total[...] += jnp.dot(turned[owner], right, preferred_element_type=F32)

    reached(1)
    reach(2)
    second.second()
    share_rows(0).start()
    heads_all(heads.at[1, pl.ds(0, width // 2)], 0).wait_recv()
    for side in range(2):
        head_copy(side, 1).start()
    logits(0, 0)
    heads_all(heads.at[1, pl.ds(0, width // 2)], 1).wait_recv()
    logits(0, 1)
    statistics(0)
    send_plane(0)
    second.third()
    reached(2)
    send_depth(0)
    second.fourth()

    @pl.when(holds_rows)
    def _():
        mate_copy(extra.at[context], extra.at[context], 2).wait_recv()

    @pl.when(jnp.logical_not(holds_rows))
    def _():
        local_copy(extra.at[context], extra.at[context], 2).wait()

    second.finish()
    third.begin()
    share_rows(1).start()
    logits(1, 0)
    logits(1, 1)
    statistics(1)
    send_plane(1)
    third.second()
    gaps(0)
    send_depth(1)
    third.third()
    own_grad(0)
    share_rows(0).wait_recv()
    mate_grad(0)
    third.fourth()
    low_all.wait_recv()
    extra_grad(0)
    gaps(1)

    def kl_copy(number, source_core):
        device = (sequence, (z, below)[number], context)
        return pltpu.make_async_remote_copy(
            src_ref=kl_own, dst_ref=kl_in.at[source_core], send_sem=kl_send.at[number],
            recv_sem=kl_recv.at[number], device_id=device, device_id_type=MESH,
        )

    kl_copy(1, core).start()

    @pl.when(jnp.logical_not(holds_rows))
    def _():
        kl_copy(0, core).start()

    own_grad(1)
    share_rows(1).wait_recv()
    mate_grad(1)

    @pl.when(holds_rows)
    def _():
        kl_copy(0, other).wait_recv()
        kl_in[core] = kl_own[...]

    @pl.when(jnp.logical_not(holds_rows))
    def _():
        pltpu.make_async_remote_copy(
            src_ref=kl_in, dst_ref=kl_in, send_sem=kl_send.at[1], recv_sem=kl_recv.at[1],
            device_id=mate, device_id_type=MESH,
        ).wait_recv()

    lane = lax.broadcasted_iota(jnp.int32, (8, count), 1)
    token_kl = jnp.zeros((8, count), F32)
    for owner in range(2):
        for group in range(2):
            start = (owner * 2 + group) * RUN
            moved = pltpu.roll(kl_in[owner, group], lax.rem(start - context * RUN + count, count), 1)
            token_kl = jnp.where((lane >= start) & (lane < start + RUN), moved, token_kl)
    kl_ref[...] = token_kl[0:1, 0:4 * RUN]

    third.finish()
    for owner in range(2):
        turned[owner] = jnp.transpose(extra[:, owner * RUN:(owner + 1) * RUN, :].reshape(count, part))
    extra_grad(1)
    grad_ref[...] = total[...].astype(grad_ref.dtype)

    first.sent()
    second.sent()
    third.sent()
    low_all.wait_send()
    heads_all(heads.at[1], 0).wait_send()

    @pl.when(holds_rows)
    def _():
        two = rows.at[0, pl.ds(0, 2 * RUN), :]
        mate_copy(two, two, 0).wait_send()

    @pl.when(jnp.logical_not(holds_rows))
    def _():
        mate_copy(extra.at[context], extra.at[context], 2).wait_send()
        kl_copy(0, core).wait_send()

    kl_copy(1, core).wait_send()
    for group in range(2):
        share_rows(group).wait_send()
        for kind in range(4):
            stat_all(group, kind).wait_send()
        gap_all(group, 3).wait_send()


def settle(kl_ref, grad_ref, kl_out, grad_out, sem):
    copies = [
        pltpu.make_async_copy(grad_ref, grad_out, sem.at[0]),
        pltpu.make_async_copy(kl_ref, kl_out, sem.at[1]),
    ]
    for copy in copies:
        copy.start()
    for copy in copies:
        copy.wait()


def local(depth, teacher_hidden, draft_hidden, teacher_head, draft_head):
    teach_width, vocab = teacher_head.shape
    draft_width = draft_head.shape[0]
    width, part = teach_width + draft_width, draft_width // 2
    count, levels = PLANE * RUN, depth // 2
    own_rows = teacher_hidden.shape[0]
    dma = pltpu.SemaphoreType.DMA
    scratch = [
        pltpu.VMEM((2, count, width), BF16),
        pltpu.VMEM((2, width, vocab), BF16),
        pltpu.VMEM((PLANE, own_rows // 2, part), BF16),
        pltpu.VMEM((2, count, part), BF16),
        pltpu.VMEM((2, count, part), BF16),
        pltpu.VMEM((2, count, 2 * vocab), F32),
        pltpu.VMEM((2, count, 2 * vocab), F32),
        pltpu.VMEM((count, 128), F32),
        pltpu.VMEM((2, PLANE, 8, 128), F32),
        pltpu.VMEM((2, levels, 8, 128), F32),
        pltpu.VMEM((2, PLANE, 8, 128), F32),
        pltpu.VMEM((2, levels, 8, 128), F32),
        pltpu.VMEM((128, count), F32),
        pltpu.VMEM((2, count, vocab), BF16),
        pltpu.VMEM((2, 2, count, vocab // 2), BF16),
        pltpu.VMEM((2, count, vocab), BF16),
        pltpu.VMEM((4, count, vocab), BF16),
        pltpu.VMEM((2, part, count), BF16),
        pltpu.VMEM((2, 8, count), F32),
        pltpu.VMEM((2, 2, 8, count), F32),
        pltpu.VMEM((part, vocab), F32),
        pltpu.SemaphoreType.REGULAR((3,)),
        dma((4,)),
        dma((1,)), dma((1,)),
        dma((3,)), dma((3, 12)),
        dma((1,)), dma((2,)),
        dma((2,)), dma((2,)),
        dma((1,)), dma((3,)),
        dma((2, 4)), dma((2, 4)),
        dma((2,)), dma((2, 2)),
        dma((2,)), dma((2,)),
    ]
    token_kl, head_grad = pl.pallas_call(
        functools.partial(kernel, depth),
        out_shape=(pltpu.VMEM((1, own_rows), F32), pltpu.VMEM((part, vocab), BF16)),
        in_specs=[pl.BlockSpec(memory_space=pl.ANY)] * 4,
        out_specs=(pl.BlockSpec(memory_space=pltpu.VMEM), pl.BlockSpec(memory_space=pltpu.VMEM)),
        scratch_shapes=scratch,
        compiler_params=pltpu.CompilerParams(collective_id=0, has_side_effects=True, vmem_limit_bytes=60 << 20),
        name="distill",
    )(teacher_hidden, draft_hidden, teacher_head, draft_head)
    token_kl, head_grad = pl.pallas_call(
        settle,
        out_shape=(pltpu.HBM((1, own_rows), F32), pltpu.HBM((part, vocab), BF16)),
        in_specs=[pl.BlockSpec(memory_space=pltpu.VMEM)] * 2,
        out_specs=(pl.BlockSpec(memory_space=pltpu.HBM), pl.BlockSpec(memory_space=pltpu.HBM)),
        scratch_shapes=[pltpu.SemaphoreType.DMA((2,))],
        compiler_params=pltpu.CompilerParams(vmem_limit_bytes=8 << 20),
        name="settle",
    )(token_kl, head_grad)
    return token_kl.reshape(own_rows), head_grad


def solution(mesh):
    in_specs = (
        P(("dp", "context"), None),
        P(("dp", "context"), None),
        P(None, ("tensor", "context")),
        P(None, ("tensor", "context")),
    )
    out_specs = (P(("dp", "context")), P("dp", ("tensor", "context")))
    return jax.shard_map(
        functools.partial(local, mesh.shape["tensor"]), mesh=mesh, in_specs=in_specs, out_specs=out_specs, check_vma=False
    )
```
